32 devices in a mesh: clips: 2 (over y), tm: 4 (over x, core), rows: 4 (over z).
Axes of the slice: x: 2, y: 2, z: 4, core: 2. Of those that a mesh axis runs over, the one named last changes fastest.
Arguments:
- features: bfloat16 [8, 8, 48, 384], P(('clips', 'tm'), 'rows'), parts along dimension 0, may hold values from -320 to 320
- first_gain: float32 [384], replicated, may hold values from 0.5 to 1.5
- first_shift: float32 [384], replicated, may hold values from -3 to 3
- first_kernel: bfloat16 [384, 3, 3, 3, 384], P('tm'), may hold values from -0.0625 to 0.0625
- first_bias: float32 [384], P('tm'), may hold values from -2 to 2
- second_gain: float32 [384], replicated, may hold values from 0.5 to 1.5
- second_shift: float32 [384], replicated, may hold values from -3 to 3
- second_kernel: bfloat16 [384, 3, 3, 3, 384], P('tm'), may hold values from -0.0625 to 0.0625
- second_bias: float32 [384], P('tm'), may hold values from -2 to 2
- third_gain: float32 [384], replicated, may hold values from 0.5 to 1.5
- third_shift: float32 [384], replicated, may hold values from -3 to 3
- query_weight: bfloat16 [384, 384], replicated, may hold values from -0.30618622 to 0.30618622
- key_weight: bfloat16 [384, 384], replicated, may hold values from -1.8371173 to 1.8371173
- value_weight: bfloat16 [384, 384], replicated, may hold values from -0.3125 to 0.3125
- output_weight: bfloat16 [384, 384], replicated, may hold values from -0.3125 to 0.3125
Outputs:
- decoded: bfloat16 [8, 8, 48, 384], P(('clips', 'tm'), 'rows'), parts along dimension 0
The draws below stay inside these ranges and needn't reach their ends.
There are 2 independent parts, one for each index of `clips`. The reference program is written for one: setup_inputs(seed, part) draws one part's arguments, and reference() takes and returns one part's arrays. A program takes and returns all parts, laid end to end along the dimension named above; an argument that names none is the same for every part. Nothing has to cross between parts.
All inputs are finite; a program needn't handle non-finite values.
Results may differ from the reference program's by a relative error of at most 0.029.
Values may be sent and summed in bfloat16 or wider, within the bound.
A program may use at most 64 MiB of HBM per device.

```python
import jax
import jax.numpy as jnp
from jax import lax

C = 384
GROUPS = 32
WIDTH = 48
HEIGHT = 8
FRAMES = 4


def draw_features(key, part):
    base = jnp.clip(jax.random.normal(jax.random.fold_in(key, 1), (FRAMES, HEIGHT, WIDTH, C), jnp.float32), -6.0, 6.0)
    ramp = jnp.arange(HEIGHT, dtype=jnp.float32) / max(HEIGHT - 1, 1)
    rough = jnp.exp(jax.random.uniform(jax.random.fold_in(key, 3), (HEIGHT,), jnp.float32) * jnp.log(20.0)) / 20.0
    level = ((1.0 + 2.0 * ramp) * rough)[None, :, None, None]
    value = 0.5 * base * level
    return jnp.clip(value, -320.0, 320.0).astype(jnp.bfloat16)


def attention_pair(key):
    first = jnp.clip(jax.random.normal(jax.random.fold_in(key, 11), (C, C), jnp.float32), -6.0, 6.0) * C ** (-0.5)
    noise = jnp.clip(jax.random.normal(jax.random.fold_in(key, 12), (C, C), jnp.float32), -6.0, 6.0) * C ** (-0.5)
    second = noise
    return (first, second)


def draw_query_weight(key, part):
    return attention_pair(key)[0].astype(jnp.bfloat16)


def draw_key_weight(key, part):
    return attention_pair(key)[1].astype(jnp.bfloat16)


def levels(stream_key, shape, split, smallest, high):
    loudness, own = 1.0, jax.random.fold_in(stream_key, 6)
    for axis_at, shards_of in split:
        heights = jnp.exp(jax.random.uniform(jax.random.fold_in(own, axis_at), (shards_of,), jnp.float32, smallest / len(split), high / len(split)))
        loudness = loudness * jnp.repeat(heights, shape[axis_at] // shards_of).reshape([-1 if axis == axis_at else 1 for axis in range(len(shape))])
    return loudness


def normal_values(key, dims, scale, reach, pieces=(), held_as=jnp.bfloat16):
    factor_of = levels(key, dims, pieces, -0.22, 0.18) if pieces else 1.0
    result = jax.random.normal(key, dims, jnp.float32) * scale * factor_of
    return jnp.minimum(jnp.maximum(result, -reach), reach).astype(held_as)


def setup_inputs(seed: int = 0, part: int = 0) -> dict:
    key_list = jax.random.split(jax.random.key(seed), 16)
    part_splits = jax.random.split(jax.random.fold_in(key_list[15], part), 16)
    return {
        "features": draw_features(jax.random.fold_in(jax.random.fold_in(key_list[15], part), 71), part),
        "first_gain": jnp.clip(1.0 + 0.1 * jax.random.normal(key_list[1], (C,), jnp.float32), 0.5, 1.5),
        "first_shift": normal_values(key_list[2], (C,), 0.5, 3.0, (), jnp.float32),
        "first_kernel": normal_values(key_list[3], (C, 3, 3, 3, C), (27 * C) ** -0.5, 0.0625, ((0, 4),)),
        "first_bias": normal_values(key_list[4], (C,), 0.3, 2.0, ((0, 4),), jnp.float32),
        "second_gain": jnp.clip(1.0 + 0.1 * jax.random.normal(key_list[5], (C,), jnp.float32), 0.5, 1.5),
        "second_shift": normal_values(key_list[6], (C,), 0.5, 3.0, (), jnp.float32),
        "second_kernel": normal_values(key_list[7], (C, 3, 3, 3, C), (27 * C) ** -0.5, 0.0625, ((0, 4),)),
        "second_bias": normal_values(key_list[8], (C,), 0.3, 2.0, ((0, 4),), jnp.float32),
        "third_gain": jnp.clip(1.0 + 0.1 * jax.random.normal(key_list[9], (C,), jnp.float32), 0.5, 1.5),
        "third_shift": normal_values(key_list[10], (C,), 0.5, 3.0, (), jnp.float32),
        "query_weight": draw_query_weight(jax.random.fold_in(key_list[15], 71), part),
        "key_weight": draw_key_weight(jax.random.fold_in(key_list[15], 71), part),
        "value_weight": normal_values(key_list[13], (C, C), C ** -0.5, 0.3125),
        "output_weight": normal_values(key_list[14], (C, C), C ** -0.5, 0.3125),
    }


epsilon = 1e-06

def group_norm(values, gain, shift):
    frame_count, row_count, col_count, channels = values.shape
    grouped = values.reshape(frame_count, row_count, col_count, GROUPS, channels // GROUPS)
    average = lax.optimization_barrier(jnp.mean(grouped, axis=(1, 2, 4), keepdims=True))
    variance = lax.optimization_barrier(jnp.mean(jnp.square(grouped - average), axis=(1, 2, 4), keepdims=True))
    normal_part = ((grouped - average) / jnp.sqrt(variance + epsilon)).reshape(frame_count, row_count, col_count, channels)
    return normal_part * gain + shift

def causal_conv(active, kernel, bias):
    frame_count, row_count, col_count, channels = active.shape
    outputs = kernel.shape[0]
    padded = jnp.pad(active, ((2, 0), (1, 1), (1, 1), (0, 0)))
    summed = jnp.zeros((frame_count * row_count * col_count, outputs), jnp.float32)
    for tap_time in range(3):
        for tap_row in range(3):
            window = padded[tap_time:tap_time + frame_count, tap_row:tap_row + row_count]
            stacked = jnp.concatenate([window[:, :, shift_col:shift_col + col_count] for shift_col in range(3)], axis=-1)
            tap_weight = kernel[:, tap_time, tap_row].reshape(outputs, 3 * channels)
            summed = summed + lax.dot_general(stacked.reshape(-1, 3 * channels), tap_weight, (((1,), (1,)), ((), ())), preferred_element_type=jnp.float32)
    summed = summed + bias
    return summed.reshape(frame_count, row_count, col_count, -1).astype(jnp.bfloat16)

def frame_attention(inputs):
    queries, keys, values = inputs
    scores = jnp.dot(queries, keys.T, preferred_element_type=jnp.float32)
    peak = lax.optimization_barrier(jnp.max(scores, axis=-1, keepdims=True))
    expon = jnp.exp(scores - peak)
    total = lax.optimization_barrier(jnp.sum(expon, axis=-1, keepdims=True))
    summed = jnp.dot(expon.astype(jnp.bfloat16), values, preferred_element_type=jnp.float32)
    return (summed / total).astype(jnp.bfloat16)

def reference(features, first_gain, first_shift, first_kernel, first_bias, second_gain, second_shift, second_kernel, second_bias, third_gain, third_shift, query_weight, key_weight, value_weight, output_weight):
    frame_count, row_count, col_count, channels = features.shape
    start = features.astype(jnp.float32)
    active1 = jax.nn.silu(group_norm(start, first_gain, first_shift)).astype(jnp.bfloat16)
    conv1 = causal_conv(active1, first_kernel, first_bias)
    active2 = jax.nn.silu(group_norm(conv1.astype(jnp.float32), second_gain, second_shift)).astype(jnp.bfloat16)
    conv2 = causal_conv(active2, second_kernel, second_bias)
    hidden = (start + conv2.astype(jnp.float32)).astype(jnp.bfloat16)
    normed = group_norm(hidden.astype(jnp.float32), third_gain, third_shift).astype(jnp.bfloat16)
    flat = normed.reshape(-1, channels)
    queries = (jnp.dot(flat, query_weight, preferred_element_type=jnp.float32) * C ** (-0.5)).astype(jnp.bfloat16)
    keys = jnp.dot(flat, key_weight, preferred_element_type=jnp.float32).astype(jnp.bfloat16)
    values = jnp.dot(flat, value_weight, preferred_element_type=jnp.float32).astype(jnp.bfloat16)
    shape3 = (frame_count, row_count * col_count, channels)
    attended = lax.map(frame_attention, (queries.reshape(shape3), keys.reshape(shape3), values.reshape(shape3)))
    projected = jnp.dot(attended.reshape(-1, channels), output_weight, preferred_element_type=jnp.float32)
    decoded = hidden.astype(jnp.float32).reshape(-1, channels) + projected
    return decoded.astype(jnp.bfloat16).reshape(frame_count, row_count, col_count, channels)
```

```python
import functools

import jax
import jax.numpy as jnp
from jax import lax
from jax.experimental import pallas as pl
from jax.experimental.pallas import tpu as pltpu
from jax.sharding import PartitionSpec as P

GROUPS = 32
EPS = 1e-06
LANES = 128
MESH = pl.DeviceIdType.MESH
F32 = jnp.float32
BF16 = jnp.bfloat16
NT = (((1,), (1,)), ((), ()))


def flat(ref):
    return ref[...].reshape(1, ref.shape[0])


def padded(ref):
    row = flat(ref)
    rest = LANES - ref.shape[0]
    return jnp.concatenate([row, jnp.zeros((1, rest), F32)], axis=1) if rest else row


def each(count, body):
    if count <= 16:
        for n in range(count):
            body(n)
    else:
        lax.fori_loop(0, count, lambda n, c: (body(n), c)[1], 0)


def membership(size, per_group):
    a = lax.broadcasted_iota(jnp.int32, (size, size), 0) // per_group
    b = lax.broadcasted_iota(jnp.int32, (size, size), 1) // per_group
    return jnp.where(a == b, 1.0, 0.0).astype(BF16)


def group_sum(rows, member):
    hi = rows.astype(BF16).astype(F32)
    rest = rows - hi
    mid = rest.astype(BF16).astype(F32)
    low = rest - mid
    count = rows.shape[0]
    terms = jnp.concatenate([hi, mid, low], axis=0).astype(BF16)
    out = jnp.dot(terms, member, preferred_element_type=F32)
    return out[:count] + out[count : 2 * count] + out[2 * count :]


def block_stats(blocks, member, entries):
    sums = jnp.concatenate([jnp.sum(b, axis=0, keepdims=True) for b in blocks], axis=0)
    means = group_sum(sums, member) / entries
    squares = []
    for n, b in enumerate(blocks):
        d = b - means[n : n + 1]
        squares.append(jnp.sum(d * d, axis=0, keepdims=True))
    return means, group_sum(jnp.concatenate(squares, axis=0), member)


def merge_stats(means, squares, entries):
    count = len(means)
    mean = functools.reduce(lambda a, b: a + b, means) / count
    total = functools.reduce(lambda a, b: a + b, squares)
    for m in means:
        d = m - mean
        total = total + entries * (d * d)
    return mean, lax.rsqrt(total / (count * entries) + EPS)


def kernel(T, R, W, rows, C, OUT,
           feath, g1h, s1h, w1h, b1h, g2h, s2h, w2h, b2h, g3h, s3h, wqh, wkh, wvh, woh,
           out,
           feat, g1, s1, g2, s2, g3, s3, b1, b2, xin, y1, cols, w1, w2, aw, st1, st2, hs, hfull, normed,
           lsem, blk_s, blk_r, top_s, top_r, bot_s, bot_r, st_s, st_r, hid_s, hid_r):
    t = lax.axis_index("tm")
    z = lax.axis_index("rows")
    me = t * R + z
    N = T * R
    RP = rows * W
    EXT = (rows + 2) * W
    per = C // GROUPS
    entries = RP * per

    loads = [
        pltpu.make_async_copy(w1h, w1.at[:, pl.ds(0, OUT), :], lsem.at[0]),
        pltpu.make_async_copy(w2h, w2.at[:, pl.ds(0, OUT), :], lsem.at[1]),
    ] + [
        pltpu.make_async_copy(src, aw.at[n], lsem.at[2 + n])
        for n, src in enumerate((wqh, wkh, wvh, woh))
    ]
    small = [
        pltpu.make_async_copy(src, dst, lsem.at[6 + n])
        for n, (src, dst) in enumerate((
            (feath, feat), (g1h, g1), (s1h, s1), (g2h, g2), (s2h, s2), (g3h, g3), (s3h, s3),
            (b1h, b1), (b2h, b2)))
    ]
    for load in small + loads:
        load.start()

    def peer(p):
        other = lax.rem(me + p, N)
        return other // R, lax.rem(other, R)

    barrier = pltpu.get_barrier_semaphore()

    def greet(n):
        pt, pz = peer(n + 1)
        pl.semaphore_signal(barrier, inc=1, device_id={"tm": pt, "rows": pz}, device_id_type=MESH)

    each(N - 1, greet)

    def remote(src, dst, ssem, rsem, pt, pz):
        return pltpu.make_async_remote_copy(
            src_ref=src, dst_ref=dst, send_sem=ssem, recv_sem=rsem,
            device_id={"tm": pt, "rows": pz}, device_id_type=MESH)

    for load in small:
        load.wait()
    x = feat[...].astype(F32)
    member = membership(C, per)
    mean, square = block_stats([x], member, entries)
    st1[me] = jnp.concatenate([mean, square], axis=0)
    if OUT < LANES:
        w1[:, OUT:, :] = jnp.zeros((27, LANES - OUT, C), BF16)
        w2[:, OUT:, :] = jnp.zeros((27, LANES - OUT, C), BF16)

    pl.semaphore_wait(barrier, N - 1)

    def stat_copy(phase, ref, n):
        pt, pz = peer(n + 1)
        return remote(ref.at[me], ref.at[me], st_s.at[phase, n], st_r.at[phase, me], pt, pz)

    def stat_arrival(phase, ref, n):
        pt, pz = peer(n + 1)
        src = pt * R + pz
        return remote(ref.at[src], ref.at[src], st_s.at[phase, n], st_r.at[phase, src], pt, pz)

    core = lax.rem(t, 2)
    sib = t + 1 - 2 * core
    X = T // 2
    chip = t // 2

    def same(n):
        return 2 * lax.rem(chip + n, X) + core

    def other(n):
        return 2 * lax.rem(chip + n, X) + 1 - core

    def pieces(phase, body, first, last, at):
        blocks = [remote(body, at(t, W, RP), blk_s.at[phase, n], blk_r.at[phase, t], same(n), z)
                  for n in range(1, X)]
        blocks.append(remote(body, at(t, W, RP), blk_s.at[phase, 0], blk_r.at[phase, t], sib, z))
        down = [remote(last, at(t, 0, W), top_s.at[phase, n], top_r.at[phase, t], same(n), z + 1)
                for n in range(X)]
        up = [remote(first, at(t, W + RP, W), bot_s.at[phase, n], bot_r.at[phase, t], same(n), z - 1)
              for n in range(X)]
        return blocks, down, up

    def gather_start(*args):
        blocks, down, up = pieces(*args)
        for c in blocks:
            c.start()

        @pl.when(z + 1 < R)
        def _():
            for c in down[1:] + down[:1]:
                c.start()

        @pl.when(z > 0)
        def _():
            for c in up[1:] + up[:1]:
                c.start()

    def forward(phase, at, sems, offset, count, src, n):
        ssem, rsem = sems
        return remote(at(src, offset, count), at(src, offset, count),
                      ssem.at[phase, X + n], rsem.at[phase, src], sib, z)

    blk, top, bot = (blk_s, blk_r), (top_s, top_r), (bot_s, bot_r)
    forwards = ((blk, W, RP, 1), (top, 0, W, 0), (bot, W + RP, W, 0))

    def relay(phase, at, which):
        sems, offset, count, start = forwards[which]
        for n in range(start, X):
            c = forward(phase, at, sems, offset, count, same(n), n)
            c.wait_recv()
            c.start()

    def sibling_wait(phase, at, which):
        sems, offset, count, _ = forwards[which]
        for n in range(X):
            forward(phase, at, sems, offset, count, other(n), n).wait_recv()

    def gather_sent(*args):
        phase, at = args[0], args[4]
        blocks, down, up = pieces(*args)
        for c in blocks:
            c.wait_send()
        for n in range(1, X):
            forward(phase, at, blk, W, RP, same(n), n).wait_send()

        @pl.when(z + 1 < R)
        def _():
            for c in down:
                c.wait_send()
            for n in range(X):
                forward(phase, at, bot, W + RP, W, same(n), n).wait_send()

        @pl.when(z > 0)
        def _():
            for c in up:
                c.wait_send()
            for n in range(X):
                forward(phase, at, top, 0, W, same(n), n).wait_send()

    def put_columns(f, offset, value):
        count = value.shape[0]
        active = value * (0.5 * jnp.tanh(0.5 * value) + 0.5)
        col = lax.rem(lax.broadcasted_iota(jnp.int32, (count, C), 0), W)
        before = jnp.where(col == 0, 0.0, pltpu.roll(active, 1, 0))
        after = jnp.where(col == W - 1, 0.0, pltpu.roll(active, count - 1, 0))
        cols[f, pl.ds(offset, count), 0:C] = before.astype(BF16)
        cols[f, pl.ds(offset, count), C : 2 * C] = active.astype(BF16)
        cols[f, pl.ds(offset, count), 2 * C : 3 * C] = after.astype(BF16)

    def conv(weights):
        parts = {}
        for i in range(3):
            frames = T - (2 - i)
            if frames <= 0:
                continue
            total = None
            for j in range(3):
                for k in range(3):
                    window = cols[0:frames, j * W : j * W + RP, k * C : (k + 1) * C]
                    term = lax.dot_general(
                        window.reshape(frames * RP, C), weights[(i * 3 + j) * 3 + k], NT,
                        preferred_element_type=F32)
                    total = term if total is None else total + term
            parts[i] = total
        results = []
        for f in range(T):
            value = parts[2][f * RP : (f + 1) * RP]
            for i in (0, 1):
                src = f + i - 2
                if src >= 0:
                    value = value + parts[i][src * RP : (src + 1) * RP]
            results.append(value)
        return results

    zero_row = jnp.zeros((W, 3 * C), BF16)

    at1 = lambda src, offset, count: xin.at[src, pl.ds(offset, count), :]
    phase1 = (0, feat, feat.at[pl.ds(0, W), :], feat.at[pl.ds(RP - W, W), :], at1)
    each(N - 1, lambda n: stat_copy(0, st1, n).start())
    gather_start(*phase1)
    xin[t, W : W + RP, :] = feat[...]
    each(N - 1, lambda n: stat_arrival(0, st1, n).wait_recv())

    gain1, shift1 = flat(g1), flat(s1)

    def norm1(f):
        means = [st1[f * R + r, 0:1, :] for r in range(R)]
        squares = [st1[f * R + r, 1:2, :] for r in range(R)]
        mean, inv = merge_stats(means, squares, entries)
        return mean, inv * gain1

    def fill1(f, offset, count):
        mean, scale = norm1(f)
        value = (xin[f, pl.ds(offset, count), :].astype(F32) - mean) * scale + shift1
        put_columns(f, offset, value)

    fill1(t, W, RP)
    relay(0, at1, 0)

    @pl.when(z > 0)
    def _():
        relay(0, at1, 1)

    @pl.when(z + 1 < R)
    def _():
        relay(0, at1, 2)

    for n in range(1, X):
        fill1(same(n), W, RP)
    sibling_wait(0, at1, 0)
    for n in range(X):
        fill1(other(n), W, RP)

    @pl.when(z > 0)
    def _():
        sibling_wait(0, at1, 1)
        for f in range(T):
            fill1(f, 0, W)

    @pl.when(z == 0)
    def _():
        for f in range(T):
            cols[f, 0:W, :] = zero_row

    @pl.when(z + 1 < R)
    def _():
        sibling_wait(0, at1, 2)
        for f in range(T):
            fill1(f, W + RP, W)

    @pl.when(z + 1 == R)
    def _():
        for f in range(T):
            cols[f, W + RP : EXT, :] = zero_row

    loads[0].wait()
    bias1 = padded(b1)
    outs = [(v + bias1).astype(BF16) for v in conv(w1)]
    member_out = membership(LANES, per)
    for f in range(T):
        y1[t, f, W : W + RP, :] = outs[f]
    mean, square = block_stats([v.astype(F32) for v in outs], member_out, entries)
    st2[me, 0] = mean
    st2[me, 1] = square

    at2 = lambda src, offset, count: y1.at[src, :, pl.ds(offset, count), :]
    phase2 = (1, at2(t, W, RP), at2(t, W, W), at2(t, RP, W), at2)
    each(N - 1, lambda n: stat_copy(1, st2, n).start())
    gather_start(*phase2)

    pick = jnp.where(
        (lax.broadcasted_iota(jnp.int32, (C, LANES), 0)
         == t * OUT + lax.broadcasted_iota(jnp.int32, (C, LANES), 1))
        & (lax.broadcasted_iota(jnp.int32, (C, LANES), 1) < OUT), 1.0, 0.0).astype(BF16)
    own = jnp.dot(xin[:, W : W + RP, :].reshape(T * RP, C), pick, preferred_element_type=F32)

    each(N - 1, lambda n: stat_arrival(1, st2, n).wait_recv())
    gain2, shift2 = flat(g2), flat(s2)
    mean_cols, inv_cols = [], []
    for s in range(T):
        mean, inv = merge_stats(
            [st2[s * R + r, 0] for r in range(R)], [st2[s * R + r, 1] for r in range(R)], entries)
        mean_cols.append(mean[:, :OUT])
        inv_cols.append(inv[:, :OUT])
    mean2 = jnp.concatenate(mean_cols, axis=1)
    scale2 = jnp.concatenate(inv_cols, axis=1) * gain2

    def joined(blocks):
        return jnp.concatenate([b.astype(F32)[:, :OUT] for b in blocks], axis=1)

    def fill2(f, offset, count):
        raw = joined([y1[s, f, offset : offset + count, :] for s in range(T)])
        value = (raw - mean2[f : f + 1]) * scale2[f : f + 1] + shift2
        put_columns(f, offset, value)

    relay(1, at2, 0)

    @pl.when(z > 0)
    def _():
        relay(1, at2, 1)

    @pl.when(z + 1 < R)
    def _():
        relay(1, at2, 2)

    sibling_wait(1, at2, 0)
    for f in range(T):
        fill2(f, W, RP)

    @pl.when(z > 0)
    def _():
        sibling_wait(1, at2, 1)
        for f in range(T):
            fill2(f, 0, W)

    @pl.when(z + 1 < R)
    def _():
        sibling_wait(1, at2, 2)
        for f in range(T):
            fill2(f, W + RP, W)

    loads[1].wait()
    bias2 = padded(b2)
    for f, v in enumerate(conv(w2)):
        rounded = (v + bias2).astype(BF16).astype(F32)
        hs[f] = (own[f * RP : (f + 1) * RP] + rounded).astype(BF16)

    def place(src, zz):
        return hfull.at[src, pl.ds(pl.multiple_of(zz * RP, 16), RP), :]

    def hidden_copy(n):
        pt, pz = peer(n + 1)
        return remote(hs.at[pt], place(t, z), hid_s.at[n], hid_r.at[me], pt, pz)

    def hidden_arrival(n):
        pt, pz = peer(n + 1)
        return remote(place(pt, pz), place(pt, pz), hid_s.at[n], hid_r.at[pt * R + pz], pt, pz)

    each(N - 1, lambda n: hidden_copy(n).start())
    hfull[t, pl.ds(pl.multiple_of(z * RP, 16), RP), :] = hs[t]

    each(N - 1, lambda n: stat_copy(0, st1, n).wait_send())
    gather_sent(*phase1)
    each(N - 1, lambda n: stat_copy(1, st2, n).wait_send())
    gather_sent(*phase2)
    for n in range(2, 6):
        loads[n].wait()

    each(N - 1, lambda n: hidden_arrival(n).wait_recv())

    total_rows = R * RP
    chunk = min(total_rows, 4 * RP)
    parts = total_rows // chunk

    def frame_rows(n):
        start = pl.multiple_of(n * chunk, 16)
        return joined([hfull[s, pl.ds(start, chunk), :] for s in range(T)])

    def fold(body, init):
        if parts == 1:
            return body(0, init)
        return lax.fori_loop(0, parts, body, init)

    zero = jnp.zeros((1, C), F32)
    sums = fold(lambda n, a: a + jnp.sum(frame_rows(n), axis=0, keepdims=True), zero)
    mean = group_sum(sums, member) / (entries * R)

    def deviation(n, a):
        d = frame_rows(n) - mean
        return a + jnp.sum(d * d, axis=0, keepdims=True)

    var = group_sum(fold(deviation, zero), member) / (entries * R)
    scale3 = lax.rsqrt(var + EPS) * flat(g3)
    shift3 = flat(s3)

    def normalise(n, c):
        start = pl.multiple_of(n * chunk, 16)
        value = ((frame_rows(n) - mean) * scale3 + shift3).astype(BF16)
        normed[0, pl.ds(start, chunk), :] = value
        normed[1, pl.ds(start, chunk), :] = jnp.dot(value, aw[1], preferred_element_type=F32).astype(BF16)
        normed[2, pl.ds(start, chunk), :] = jnp.dot(value, aw[2], preferred_element_type=F32).astype(BF16)
        return c

    fold(normalise, 0)
    mine = pl.ds(pl.multiple_of(z * RP, 16), RP)
    queries = (jnp.dot(normed[0, mine, :], aw[0], preferred_element_type=F32) * C ** (-0.5)).astype(BF16)
    scores = lax.dot_general(queries, normed[1], NT, preferred_element_type=F32)
    peak = jnp.max(scores, axis=1, keepdims=True)
    weights = jnp.exp(scores - peak)
    total = jnp.sum(weights, axis=1, keepdims=True)
    summed = jnp.dot(weights.astype(BF16), normed[2], preferred_element_type=F32)
    attended = (summed / total).astype(BF16)
    hidden = joined([hfull[s, mine, :] for s in range(T)])
    out[...] = (hidden + jnp.dot(attended, aw[3], preferred_element_type=F32)).astype(BF16)

    each(N - 1, lambda n: hidden_copy(n).wait_send())


def solution(mesh):
    T, R = mesh.shape["tm"], mesh.shape["rows"]

    def per_device(features, g1, s1, k1, b1, g2, s2, k2, b2, g3, s3, wq, wk, wv, wo):
        _, rows, W, C = features.shape
        OUT = k1.shape[0]
        RP, EXT, N = rows * W, (rows + 2) * W, T * R
        taps = lambda k: jnp.transpose(k, (1, 2, 3, 0, 4)).reshape(27, OUT, C)
        vmem = pl.BlockSpec(memory_space=pltpu.VMEM)
        hbm = pl.BlockSpec(memory_space=pltpu.HBM)
        dma = pltpu.SemaphoreType.DMA
        result = pl.pallas_call(
            functools.partial(kernel, T, R, W, rows, C, OUT),
            out_shape=pltpu.VMEM((RP, C), BF16),
            in_specs=[hbm] * 15,
            out_specs=vmem,
            scratch_shapes=[pltpu.VMEM((RP, C), BF16)] + [pltpu.VMEM((C,), F32)] * 6
            + [pltpu.VMEM((OUT,), F32)] * 2 + [
                pltpu.VMEM((T, EXT, C), BF16),
                pltpu.VMEM((T, T, EXT, LANES), BF16),
                pltpu.VMEM((T, EXT, 3 * C), BF16),
                pltpu.VMEM((27, LANES, C), BF16),
                pltpu.VMEM((27, LANES, C), BF16),
                pltpu.VMEM((4, C, C), BF16),
                pltpu.VMEM((N, 2, C), F32),
                pltpu.VMEM((N, 2, T, LANES), F32),
                pltpu.VMEM((T, RP, LANES), BF16),
                pltpu.VMEM((T, R * RP, LANES), BF16),
                pltpu.VMEM((3, R * RP, C), BF16),
                dma((15,)),
                dma((2, T)), dma((2, T)),
                dma((2, T)), dma((2, T)),
                dma((2, T)), dma((2, T)),
                dma((2, N)), dma((2, N)),
                dma((N,)), dma((N,)),
            ],
            compiler_params=pltpu.CompilerParams(
                collective_id=0, has_side_effects=True, vmem_limit_bytes=62 * 1024 * 1024),
        )(features.reshape(RP, C), g1, s1, taps(k1), b1, g2, s2,
          taps(k2), b2, g3, s3, wq, wk, wv, wo)
        return result.reshape(features.shape)

    in_specs = (
        P(("clips", "tm"), "rows", None, None), P(), P(),
        P("tm", None, None, None, None), P("tm"), P(), P(),
        P("tm", None, None, None, None), P("tm"), P(), P(), P(), P(), P(), P(),
    )
    return jax.shard_map(
        per_device, mesh=mesh, in_specs=in_specs,
        out_specs=P(("clips", "tm"), "rows", None, None), check_vma=False)
```

```python
import functools

import jax
import jax.numpy as jnp
from jax import lax
from jax.experimental import pallas as pl
from jax.experimental.pallas import tpu as pltpu
from jax.sharding import PartitionSpec as P

GROUPS = 32
EPS = 1e-06
LANES = 128
MESH = pl.DeviceIdType.MESH
F32 = jnp.float32
BF16 = jnp.bfloat16
NT = (((1,), (1,)), ((), ()))


def flat(ref):
    return ref[...].reshape(1, ref.shape[0])


def padded(ref):
    row = flat(ref)
    rest = LANES - ref.shape[0]
    return jnp.concatenate([row, jnp.zeros((1, rest), F32)], axis=1) if rest else row


def each(count, body):
    if count <= 16:
        for n in range(count):
            body(n)
    else:
        lax.fori_loop(0, count, lambda n, c: (body(n), c)[1], 0)


def membership(size, per_group):
    a = lax.broadcasted_iota(jnp.int32, (size, size), 0) // per_group
    b = lax.broadcasted_iota(jnp.int32, (size, size), 1) // per_group
    return jnp.where(a == b, 1.0, 0.0).astype(BF16)


def group_sum(rows, member):
    hi = rows.astype(BF16).astype(F32)
    rest = rows - hi
    mid = rest.astype(BF16).astype(F32)
    low = rest - mid
    count = rows.shape[0]
    terms = jnp.concatenate([hi, mid, low], axis=0).astype(BF16)
    out = jnp.dot(terms, member, preferred_element_type=F32)
    return out[:count] + out[count : 2 * count] + out[2 * count :]


def block_stats(blocks, member, entries):
    sums = jnp.concatenate([jnp.sum(b, axis=0, keepdims=True) for b in blocks], axis=0)
    means = group_sum(sums, member) / entries
    squares = []
    for n, b in enumerate(blocks):
        d = b - means[n : n + 1]
        squares.append(jnp.sum(d * d, axis=0, keepdims=True))
    return means, group_sum(jnp.concatenate(squares, axis=0), member)


def merge_stats(means, squares, entries):
    count = len(means)
    mean = functools.reduce(lambda a, b: a + b, means) / count
    total = functools.reduce(lambda a, b: a + b, squares)
    for m in means:
        d = m - mean
        total = total + entries * (d * d)
    return mean, lax.rsqrt(total / (count * entries) + EPS)


def lanes_of(count):
    return lax.broadcasted_iota(jnp.int32, (count, LANES), 1)


def pack_rows(v):
    tail = v[80:96]
    lane = lanes_of(16)
    parts = []
    for j in range(3):
        moved = pltpu.roll(tail, 96 - 32 * j, 1)
        parts.append(jnp.where(lane >= 96, moved, v[16 * j : 16 * j + 16]))
    return jnp.concatenate(parts + [v[48:80]], axis=0)


def unpack_rows(p):
    lane = lanes_of(16)
    tail = jnp.zeros((16, LANES), F32)
    for j in range(3):
        moved = pltpu.roll(p[16 * j : 16 * j + 16], 32 + 32 * j, 1)
        tail = jnp.where((lane >= 32 * j) & (lane < 32 * j + 32), moved, tail)
    return jnp.concatenate([p, tail], axis=0)


def kernel(T, R, W, rows, C, OUT,
           feath, g1h, s1h, w1h, b1h, g2h, s2h, w2h, b2h, g3h, s3h, wqh, wkh, wvh, woh,
           out,
           feat, g1, s1, g2, s2, g3, s3, b1, b2, xin, y1, cols, w1, w2, aw, st1, st2, st3, hs, hfull, hid, normed, mix, pairs, singles,
           lsem, snd, rcv, st_s, st_r, hid_s, hid_r):
    t = lax.axis_index("tm")
    z = lax.axis_index("rows")
    me = t * R + z
    N = T * R
    RP = rows * W
    EXT = (rows + 2) * W
    per = C // GROUPS
    entries = RP * per
    packed2 = y1.shape[1] < T
    packed3 = hs.shape[1] < RP

    def peer(p):
        other = lax.rem(me + p, N)
        return other // R, lax.rem(other, R)

    barrier = pltpu.get_barrier_semaphore()

    def greet(n):
        pt, pz = peer(n + 1)
        pl.semaphore_signal(barrier, inc=1, device_id={"tm": pt, "rows": pz}, device_id_type=MESH)

    small = [
        pltpu.make_async_copy(src, dst, lsem.at[n])
        for n, (src, dst) in enumerate((
            (feath, feat), (g1h, g1), (s1h, s1), (g2h, g2), (s2h, s2), (g3h, g3), (s3h, s3),
            (b1h, b1), (b2h, b2)))
    ]
    small[0].start()
    each(N - 1, greet)
    for load in small[1:]:
        load.start()

    def load_taps(src, dst, n):
        for i in range(3):
            for k in range(3):
                pltpu.make_async_copy(
                    src.at[i, :, k], dst.at[:, 2 - i, pl.ds(0, OUT), pl.ds(k * C, C)], lsem.at[n]).start()

    def taps_loaded(dst, n):
        whole = dst.at[:, :, pl.ds(0, OUT), :]
        pltpu.make_async_copy(whole, whole, lsem.at[n]).wait()

    load_taps(w1h, w1, 9)
    for n, src in enumerate((wqh, wkh, wvh, woh)):
        pltpu.make_async_copy(src, aw.at[n], lsem.at[11]).start()
    load_taps(w2h, w2, 10)

    def remote(src, dst, ssem, rsem, pt, pz):
        return pltpu.make_async_remote_copy(
            src_ref=src, dst_ref=dst, send_sem=ssem, recv_sem=rsem,
            device_id={"tm": pt, "rows": pz}, device_id_type=MESH)

    small[0].wait()
    x = feat[...].astype(F32)
    member = membership(C, per)
    mean, square = block_stats([x], member, entries)
    st1[me] = jnp.concatenate([mean, square], axis=0)
    for load in small[1:]:
        load.wait()
    if OUT < LANES:
        w1[:, :, OUT:, :] = jnp.zeros((3, 3, LANES - OUT, 3 * C), BF16)
        w2[:, :, OUT:, :] = jnp.zeros((3, 3, LANES - OUT, 3 * C), BF16)

    pl.semaphore_wait(barrier, N - 1)

    def stat_copy(phase, ref, n):
        pt, pz = peer(n + 1)
        return remote(ref.at[me], ref.at[me], st_s.at[phase], st_r.at[phase], pt, pz)

    def stat_all(phase, ref):
        most = ref.at[pl.ds(0, N - 1)]
        return remote(most, most, st_s.at[phase], st_r.at[phase], lax.rem(t + 1, T), z)

    core = lax.rem(t, 2)
    sib = t + 1 - 2 * core
    X = T // 2
    chip = t // 2

    def same(n):
        return 2 * lax.rem(chip + n, X) + core

    def other(n):
        return 2 * lax.rem(chip + n, X) + 1 - core

    BLK, TOP, BOT = 0, 1, 2
    DOWN, UP = 1, 2
    spans = ((W, RP), (0, W), (W + RP, W))

    def gather_start(phase, body, first, last, at):
        for n in range(1, X):
            remote(body, at(t, W, RP), snd.at[phase, 0], rcv.at[phase, BLK, t], same(n), z).start()
        remote(body, at(t, W, RP), snd.at[phase, 0], rcv.at[phase, BLK, t], sib, z).start()
        order = list(range(1, X)) + [0]

        @pl.when(z + 1 < R)
        def _():
            for n in order:
                remote(last, at(t, 0, W), snd.at[phase, DOWN], rcv.at[phase, TOP, t], same(n), z + 1).start()

        @pl.when(z > 0)
        def _():
            for n in order:
                remote(first, at(t, W + RP, W), snd.at[phase, UP], rcv.at[phase, BOT, t], same(n), z - 1).start()

    def forward(phase, at, which, src):
        sem = (0, UP, DOWN)[which]
        block = at(src, *spans[which])
        return remote(block, block, snd.at[phase, sem], rcv.at[phase, which, src], sib, z)

    def relay(phase, at, which, sources):
        for n in sources:
            c = forward(phase, at, which, same(n))
            c.wait_recv()
            c.start()

    def relay_rims(phase, at, sources):
        @pl.when(z > 0)
        def _():
            relay(phase, at, TOP, sources)

        @pl.when(z + 1 < R)
        def _():
            relay(phase, at, BOT, sources)

    def sibling_wait(phase, at, which):
        for n in range(X):
            forward(phase, at, which, other(n)).wait_recv()

    def gather_sent(phase, at, span_at):
        def done(block, sem):
            remote(block, block, snd.at[phase, sem], rcv.at[phase, BLK, t], sib, z).wait_send()

        done(span_at(T - 1, W, RP), 0)

        @pl.when(z + 1 < R)
        def _():
            done(span_at(T, 0, W), DOWN)

        @pl.when(z > 0)
        def _():
            done(span_at(T, 0, W), UP)

    def put_columns(f, offset, value):
        count = value.shape[0]
        active = value * (0.5 * jnp.tanh(0.5 * value) + 0.5)
        col = lax.rem(lax.broadcasted_iota(jnp.int32, (count, C), 0), W)
        before = jnp.where(col == 0, 0.0, pltpu.roll(active, 1, 0))
        after = jnp.where(col == W - 1, 0.0, pltpu.roll(active, count - 1, 0))
        cols[f, pl.ds(offset, count), 0:C] = before.astype(BF16)
        cols[f, pl.ds(offset, count), C : 2 * C] = active.astype(BF16)
        cols[f, pl.ds(offset, count), 2 * C : 3 * C] = after.astype(BF16)

    def conv(weights, taps, before):
        pair, single = before
        for j in taps:
            window = cols[:, j * W : j * W + RP, :].reshape(T * RP, 3 * C)
            term = lax.dot_general(
                window, weights[j, 0:2].reshape(2 * LANES, 3 * C), NT, preferred_element_type=F32)
            pair = term if pair is None else pair + term
            if T > 2:
                term = lax.dot_general(
                    window[: (T - 2) * RP], weights[j, 2], NT, preferred_element_type=F32)
                single = term if single is None else single + term
        return pair, single

    def keep(sums):
        pairs[...] = sums[0]
        if T > 2:
            singles[...] = sums[1]

    def kept():
        return pairs[...], (singles[...] if T > 2 else None)

    def conv_frames(pair, single):
        results = []
        for f in range(T):
            value = pair[f * RP : (f + 1) * RP, :LANES]
            if f >= 1:
                value = value + pair[(f - 1) * RP : f * RP, LANES:]
            if f >= 2:
                value = value + single[(f - 2) * RP : (f - 1) * RP]
            results.append(value)
        return results

    zero_row = jnp.zeros((W, 3 * C), BF16)

    at1 = lambda src, offset, count: xin.at[src, pl.ds(offset, count), :]
    many1 = lambda count, offset, size: xin.at[pl.ds(0, count), pl.ds(offset, size), :]
    each(N - 1, lambda n: stat_copy(0, st1, n).start())
    gather_start(0, feat, feat.at[pl.ds(0, W), :], feat.at[pl.ds(RP - W, W), :], at1)
    xin[t, W : W + RP, :] = feat[...]
    stat_all(0, st1).wait_recv()

    gain1, shift1 = flat(g1), flat(s1)

    def norm1(f):
        means = [st1[f * R + r, 0:1, :] for r in range(R)]
        squares = [st1[f * R + r, 1:2, :] for r in range(R)]
        mean, inv = merge_stats(means, squares, entries)
        return mean, inv * gain1

    def fill1(f, offset, count):
        mean, scale = norm1(f)
        value = (xin[f, pl.ds(offset, count), :].astype(F32) - mean) * scale + shift1
        put_columns(f, offset, value)

    fill1(t, W, RP)
    relay(0, at1, BLK, range(1, X))
    for n in range(1, X):
        fill1(same(n), W, RP)
    relay_rims(0, at1, (0,))
    relay_rims(0, at1, range(1, X))
    sibling_wait(0, at1, BLK)
    for n in range(X):
        fill1(other(n), W, RP)

    taps_loaded(w1, 9)
    keep(conv(w1, (1,), (None, None)))

    @pl.when(z > 0)
    def _():
        sibling_wait(0, at1, TOP)
        for f in range(T):
            fill1(f, 0, W)

    @pl.when(z == 0)
    def _():
        for f in range(T):
            cols[f, 0:W, :] = zero_row

    @pl.when(z + 1 < R)
    def _():
        sibling_wait(0, at1, BOT)
        for f in range(T):
            fill1(f, W + RP, W)

    @pl.when(z + 1 == R)
    def _():
        for f in range(T):
            cols[f, W + RP : EXT, :] = zero_row

    bias1 = padded(b1)
    acc = conv(w1, (0, 2), kept())
    outs = [(v + bias1).astype(BF16).astype(F32) for v in conv_frames(*acc)]
    member_out = membership(LANES, per)
    if packed2:
        lane = lanes_of(RP)
        for f in range(T - 1):
            moved = pltpu.roll(outs[T - 1], 96 - 32 * f, 1)
            y1[t, f, W : W + RP, :] = jnp.where(lane >= 96, moved, outs[f]).astype(BF16)
    else:
        for f in range(T):
            y1[t, f, W : W + RP, :] = outs[f].astype(BF16)

    at2 = lambda src, offset, count: y1.at[src, :, pl.ds(offset, count), :]
    many2 = lambda count, offset, size: y1.at[pl.ds(0, count), :, pl.ds(offset, size), :]
    mean, square = block_stats(outs, member_out, entries)
    st2[me, 0] = mean
    st2[me, 1] = square
    each(N - 1, lambda n: stat_copy(1, st2, n).start())
    gather_start(1, at2(t, W, RP), at2(t, W, W), at2(t, RP, W), at2)

    pick = jnp.where(
        (lax.broadcasted_iota(jnp.int32, (C, LANES), 0)
         == t * OUT + lax.broadcasted_iota(jnp.int32, (C, LANES), 1))
        & (lax.broadcasted_iota(jnp.int32, (C, LANES), 1) < OUT), 1.0, 0.0).astype(BF16)
    own = jnp.dot(xin[:, W : W + RP, :].reshape(T * RP, C), pick, preferred_element_type=F32)
    pltpu.make_async_copy(aw, aw, lsem.at[11]).wait()
    mix[0] = (lax.dot_general(aw[0], aw[1], NT, preferred_element_type=F32) * C ** (-0.5)).astype(BF16)
    mix[1] = jnp.dot(aw[2], aw[3], preferred_element_type=F32).astype(BF16)

    stat_all(1, st2).wait_recv()
    gain2, shift2 = flat(g2), flat(s2)
    mean_cols, inv_cols = [], []
    for s in range(T):
        mean, inv = merge_stats(
            [st2[s * R + r, 0] for r in range(R)], [st2[s * R + r, 1] for r in range(R)], entries)
        mean_cols.append(mean[:, :OUT])
        inv_cols.append(inv[:, :OUT])
    mean2 = jnp.concatenate(mean_cols, axis=1)
    scale2 = jnp.concatenate(inv_cols, axis=1) * gain2

    def joined(blocks):
        return jnp.concatenate([b[:, :OUT] for b in blocks], axis=1)

    def conv_out(s, f, offset, count):
        if not packed2 or f < T - 1:
            return y1[s, f, offset : offset + count, :].astype(F32)
        lane = lanes_of(count)
        value = None
        for j in range(3):
            moved = pltpu.roll(y1[s, j, offset : offset + count, :].astype(F32), 32 + 32 * j, 1)
            value = moved if value is None else jnp.where(lane >= 32 * j, moved, value)
        return value

    def fill2(f, offset, count):
        raw = joined([conv_out(s, f, offset, count) for s in range(T)])
        value = (raw - mean2[f : f + 1]) * scale2[f : f + 1] + shift2
        put_columns(f, offset, value)

    relay_rims(1, at2, (0,))
    relay(1, at2, BLK, range(1, X))
    relay_rims(1, at2, range(1, X))
    sibling_wait(1, at2, BLK)
    for f in range(T):
        fill2(f, W, RP)
    taps_loaded(w2, 10)
    keep(conv(w2, (1,), (None, None)))

    @pl.when(z > 0)
    def _():
        sibling_wait(1, at2, TOP)
        for f in range(T):
            fill2(f, 0, W)

    @pl.when(z + 1 < R)
    def _():
        sibling_wait(1, at2, BOT)
        for f in range(T):
            fill2(f, W + RP, W)

    bias2 = padded(b2)
    acc = conv(w2, (0, 2), kept())
    for f, v in enumerate(conv_frames(*acc)):
        rounded = (v + bias2).astype(BF16).astype(F32)
        value = own[f * RP : (f + 1) * RP] + rounded
        hs[f] = (pack_rows(value) if packed3 else value).astype(BF16)

    def place(zz, tt):
        return hfull.at[zz * T + tt]

    def group(zz, count):
        return hfull.at[pl.ds(zz * T, count)]

    def hidden_start(pt, pz):
        remote(hs.at[pt], place(z, t), hid_s.at[0], hid_r.at[z], pt, pz).start()

    if R <= 4:
        for d in range(R - 1, 0, -1):
            for there in (z + d, z - d):
                @pl.when((there >= 0) & (there < R))
                def _():
                    for n in range(T):
                        hidden_start(lax.rem(t + n, T), there)
        for n in range(1, T):
            hidden_start(lax.rem(t + n, T), z)
    else:
        each(N - 1, lambda n: hidden_start(*peer(n + 1)))
    hfull[z * T + t] = hs[t]

    stat_all(0, st1).wait_send()
    gather_sent(0, at1, many1)
    stat_all(1, st2).wait_send()
    gather_sent(1, at2, many2)

    def arrived(zz, count):
        block = group(zz, count)
        remote(block, block, hid_s.at[0], hid_r.at[zz], lax.rem(t + 1, T), z).wait_recv()

    def take(zz):
        pieces = [place(zz, s)[...].astype(F32) for s in range(T)]
        value = joined([unpack_rows(p) for p in pieces] if packed3 else pieces)
        mean = jnp.sum(value, axis=0, keepdims=True) * (1.0 / RP)
        d = value - mean
        hid[pl.ds(pl.multiple_of(zz * RP, 16), RP), :] = value.astype(BF16)
        st3[zz] = jnp.concatenate([mean, jnp.sum(d * d, axis=0, keepdims=True)], axis=0)

    def arrival(zz):
        @pl.when(zz == z)
        def _():
            arrived(zz, T - 1)

        @pl.when(zz != z)
        def _():
            arrived(zz, T)

    def collect(n):
        zz = lax.rem(z + n, R)
        arrival(zz)
        take(zz)

    if R == 4:
        arrived(z, T - 1)
        take(z)
        for here, order in ((0, (1, 2, 3)), (1, (2, 0, 3)), (2, (1, 3, 0)), (3, (2, 1, 0))):
            @pl.when(z == here)
            def _():
                for zz in order:
                    arrived(zz, T)
                    take(zz)
    else:
        each(R, collect)

    means = [st3[r, 0:1, :] for r in range(R)]
    mean = group_sum(functools.reduce(lambda a, b: a + b, means), member) / (per * R)
    spread = functools.reduce(lambda a, b: a + b, [st3[r, 1:2, :] for r in range(R)])
    for m in means:
        d = m - mean
        spread = spread + RP * (d * d)
    var = group_sum(spread, member) / (entries * R)
    scale3 = lax.rsqrt(var + EPS) * flat(g3)
    shift3 = flat(s3)

    def normalise(r):
        part = pl.ds(pl.multiple_of(r * RP, 16), RP)
        normed[part, :] = ((hid[part, :].astype(F32) - mean) * scale3 + shift3).astype(BF16)

    each(R, normalise)
    mine = pl.ds(pl.multiple_of(z * RP, 16), RP)
    queries = jnp.dot(normed[mine, :], mix[0], preferred_element_type=F32).astype(BF16)
    scores = lax.dot_general(queries, normed[...], NT, preferred_element_type=F32)
    peak = jnp.max(scores, axis=1, keepdims=True)
    weights = jnp.exp(scores - peak)
    total = jnp.sum(weights, axis=1, keepdims=True)
    summed = jnp.dot(weights.astype(BF16), normed[...], preferred_element_type=F32)
    attended = (summed / total).astype(BF16)
    hidden = hid[mine, :].astype(F32)
    out[...] = (hidden + jnp.dot(attended, mix[1], preferred_element_type=F32)).astype(BF16)

    most = hfull.at[pl.ds(0, N - 1)]
    remote(most, most, hid_s.at[0], hid_r.at[z], sib, z).wait_send()


def solution(mesh):
    T, R = mesh.shape["tm"], mesh.shape["rows"]

    def per_device(features, g1, s1, k1, b1, g2, s2, k2, b2, g3, s3, wq, wk, wv, wo):
        _, rows, W, C = features.shape
        OUT = k1.shape[0]
        RP, EXT, N = rows * W, (rows + 2) * W, T * R
        taps = lambda k: jnp.transpose(k, (1, 2, 3, 0, 4))
        piece = 80 if OUT == 96 and RP == 96 else RP
        vmem = pl.BlockSpec(memory_space=pltpu.VMEM)
        hbm = pl.BlockSpec(memory_space=pltpu.HBM)
        dma = pltpu.SemaphoreType.DMA
        result = pl.pallas_call(
            functools.partial(kernel, T, R, W, rows, C, OUT),
            out_shape=pltpu.VMEM((RP, C), BF16),
            in_specs=[hbm] * 15,
            out_specs=vmem,
            scratch_shapes=[pltpu.VMEM((RP, C), BF16)] + [pltpu.VMEM((C,), F32)] * 6
            + [pltpu.VMEM((OUT,), F32)] * 2 + [
                pltpu.VMEM((T, EXT, C), BF16),
                pltpu.VMEM((T, 3 if T == 4 and OUT == 96 else T, EXT, LANES), BF16),
                pltpu.VMEM((T, EXT, 3 * C), BF16),
                pltpu.VMEM((3, 3, LANES, 3 * C), BF16),
                pltpu.VMEM((3, 3, LANES, 3 * C), BF16),
                pltpu.VMEM((4, C, C), BF16),
                pltpu.VMEM((N, 2, C), F32),
                pltpu.VMEM((N, 2, T, LANES), F32),
                pltpu.VMEM((R, 2, C), F32),
                pltpu.VMEM((T, piece, LANES), BF16),
                pltpu.VMEM((N, piece, LANES), BF16),
                pltpu.VMEM((R * RP, C), BF16),
                pltpu.VMEM((R * RP, C), BF16),
                pltpu.VMEM((2, C, C), BF16),
                pltpu.VMEM((T * RP, 2 * LANES), F32),
                pltpu.VMEM((max(T - 2, 1) * RP, LANES), F32),
                dma((12,)), dma((2, 3)), dma((2, 3, T)), dma((2,)), dma((2,)), dma((1,)), dma((R,)),
            ],
            compiler_params=pltpu.CompilerParams(
                collective_id=0, has_side_effects=True, vmem_limit_bytes=62 * 1024 * 1024),
        )(features.reshape(RP, C), g1, s1, taps(k1), b1, g2, s2,
          taps(k2), b2, g3, s3, wq, wk, wv, wo)
        return result.reshape(features.shape)

    in_specs = (
        P(("clips", "tm"), "rows", None, None), P(), P(),
        P("tm", None, None, None, None), P("tm"), P(), P(),
        P("tm", None, None, None, None), P("tm"), P(), P(), P(), P(), P(), P(),
    )
    return jax.shard_map(
        per_device, mesh=mesh, in_specs=in_specs,
        out_specs=P(("clips", "tm"), "rows", None, None), check_vma=False)
```

```python
import functools

import jax
import jax.numpy as jnp
from jax import lax
from jax.experimental import pallas as pl
from jax.experimental.pallas import tpu as pltpu
from jax.sharding import PartitionSpec as P

GROUPS = 32
EPS = 1e-06
LANES = 128
MESH = pl.DeviceIdType.MESH
F32 = jnp.float32
BF16 = jnp.bfloat16
NT = (((1,), (1,)), ((), ()))


def flat(ref):
    return ref[...].reshape(1, ref.shape[0])


def padded(ref):
    row = flat(ref)
    rest = LANES - ref.shape[0]
    return jnp.concatenate([row, jnp.zeros((1, rest), F32)], axis=1) if rest else row


def each(count, body):
    if count <= 16:
        for n in range(count):
            body(n)
    else:
        lax.fori_loop(0, count, lambda n, c: (body(n), c)[1], 0)


def membership(size, per_group):
    a = lax.broadcasted_iota(jnp.int32, (size, size), 0) // per_group
    b = lax.broadcasted_iota(jnp.int32, (size, size), 1) // per_group
    return jnp.where(a == b, 1.0, 0.0).astype(BF16)


def group_sum(rows, member):
    hi = rows.astype(BF16).astype(F32)
    rest = rows - hi
    mid = rest.astype(BF16).astype(F32)
    low = rest - mid
    count = rows.shape[0]
    terms = jnp.concatenate([hi, mid, low], axis=0).astype(BF16)
    out = jnp.dot(terms, member, preferred_element_type=F32)
    return out[:count] + out[count : 2 * count] + out[2 * count :]


def block_stats(blocks, member, entries):
    sums = jnp.concatenate([jnp.sum(b, axis=0, keepdims=True) for b in blocks], axis=0)
    means = group_sum(sums, member) / entries
    squares = []
    for n, b in enumerate(blocks):
        d = b - means[n : n + 1]
        squares.append(jnp.sum(d * d, axis=0, keepdims=True))
    return means, group_sum(jnp.concatenate(squares, axis=0), member)


def merge_stats(means, squares, entries):
    count = len(means)
    mean = functools.reduce(lambda a, b: a + b, means) / count
    total = functools.reduce(lambda a, b: a + b, squares)
    for m in means:
        d = m - mean
        total = total + entries * (d * d)
    return mean, lax.rsqrt(total / (count * entries) + EPS)


def lanes_of(count):
    return lax.broadcasted_iota(jnp.int32, (count, LANES), 1)


def pack_rows(v):
    tail = v[72:96]
    lane = lanes_of(24)
    parts = []
    for j in range(3):
        moved = pltpu.roll(tail, 96 - 32 * j, 1)
        parts.append(jnp.where(lane >= 96, moved, v[24 * j : 24 * j + 24]))
    return jnp.concatenate(parts, axis=0)


def unpack_rows(p):
    lane = lanes_of(24)
    tail = jnp.zeros((24, LANES), F32)
    for j in range(3):
        moved = pltpu.roll(p[24 * j : 24 * j + 24], 32 + 32 * j, 1)
        tail = jnp.where((lane >= 32 * j) & (lane < 32 * j + 32), moved, tail)
    return jnp.concatenate([p, tail], axis=0)


def iota2(shape, axis):
    return lax.broadcasted_iota(jnp.int32, shape, axis)


def ones_where(mask):
    return jnp.where(mask, 1.0, 0.0).astype(BF16)


def merge_compact(blocks, entries):
    count = len(blocks)
    mean = functools.reduce(lambda a, b: a + b, blocks) / count
    total = functools.reduce(lambda a, b: a + b, blocks)
    for b in blocks:
        d = pltpu.roll(b - mean, GROUPS, 1)
        total = total + entries * (d * d)
    inv = lax.rsqrt(total / (count * entries) + EPS)
    return jnp.where(iota2(mean.shape, 1) < GROUPS, mean, inv)


def kernel(T, R, W, rows, C, OUT,
           feath, g1h, s1h, w1h, b1h, g2h, s2h, w2h, b2h, g3h, s3h, wqh, wkh, wvh, woh,
           out,
           feat, g1, s1, g2, s2, g3, s3, b1, b2, xin, y1, cols, w1, w2, aw, st1, st2, st3, hs, hfull, hid, normed, mix, spread1, spread2, norms,
           lsem, snd, rcv, st_s, st_r, hid_s, hid_r):
    t = lax.axis_index("tm")
    z = lax.axis_index("rows")
    me = t * R + z
    N = T * R
    RP = rows * W
    EXT = (rows + 2) * W
    per = C // GROUPS
    entries = RP * per
    packed2 = y1.shape[1] < T
    packed3 = hs.shape[1] < RP

    def peer(p):
        other = lax.rem(me + p, N)
        return other // R, lax.rem(other, R)

    barrier = pltpu.get_barrier_semaphore()

    def greet(n):
        pt, pz = peer(n + 1)
        pl.semaphore_signal(barrier, inc=1, device_id={"tm": pt, "rows": pz}, device_id_type=MESH)

    small = [
        pltpu.make_async_copy(src, dst, lsem.at[n])
        for n, (src, dst) in enumerate((
            (feath, feat), (g1h, g1), (s1h, s1), (g2h, g2), (s2h, s2), (g3h, g3), (s3h, s3),
            (b1h, b1), (b2h, b2)))
    ]
    small[0].start()
    each(N - 1, greet)
    for load in small[1:]:
        load.start()

    def load_taps(src, dst, n):
        for i in range(3):
            for k in range(3):
                pltpu.make_async_copy(
                    src.at[i, :, k], dst.at[:, 2 - i, pl.ds(0, OUT), pl.ds(k * C, C)], lsem.at[n]).start()

    def taps_loaded(dst, n):
        whole = dst.at[:, :, pl.ds(0, OUT), :]
        pltpu.make_async_copy(whole, whole, lsem.at[n]).wait()

    load_taps(w1h, w1, 9)
    for n, src in enumerate((wqh, wkh, wvh, woh)):
        pltpu.make_async_copy(src, aw.at[n], lsem.at[11]).start()
    load_taps(w2h, w2, 10)

    def remote(src, dst, ssem, rsem, pt, pz):
        return pltpu.make_async_remote_copy(
            src_ref=src, dst_ref=dst, send_sem=ssem, recv_sem=rsem,
            device_id={"tm": pt, "rows": pz}, device_id_type=MESH)

    small[0].wait()
    x = feat[...].astype(F32)
    member = membership(C, per)
    mean, square = block_stats([x], member, entries)
    first = ones_where(iota2((C, LANES), 0) == per * lax.rem(iota2((C, LANES), 1), GROUPS))
    both = group_sum(jnp.concatenate([mean, square], axis=0), first)
    st1[me] = jnp.where(iota2((1, LANES), 1) < GROUPS, both[0:1], both[1:2])
    for load in small[1:]:
        load.wait()
    if OUT < LANES:
        w1[:, :, OUT:, :] = jnp.zeros((3, 3, LANES - OUT, 3 * C), BF16)
        w2[:, :, OUT:, :] = jnp.zeros((3, 3, LANES - OUT, 3 * C), BF16)

    pl.semaphore_wait(barrier, N - 1)

    def stat_copy(phase, ref, n):
        pt, pz = peer(n + 1)
        return remote(ref.at[me], ref.at[me], st_s.at[phase], st_r.at[phase], pt, pz)

    def stat_all(phase, ref):
        most = ref.at[pl.ds(0, N - 1)]
        return remote(most, most, st_s.at[phase], st_r.at[phase], lax.rem(t + 1, T), z)

    core = lax.rem(t, 2)
    sib = t + 1 - 2 * core
    X = T // 2
    chip = t // 2

    def same(n):
        return 2 * lax.rem(chip + n, X) + core

    def other(n):
        return 2 * lax.rem(chip + n, X) + 1 - core

    BLK, TOP, BOT = 0, 1, 2
    DOWN, UP = 1, 2
    spans = ((W, RP), (0, W), (W + RP, W))

    def gather_start(phase, body, first, last, at):
        for n in range(1, X):
            remote(body, at(t, W, RP), snd.at[phase, 0], rcv.at[phase, BLK, t], same(n), z).start()
        remote(body, at(t, W, RP), snd.at[phase, 0], rcv.at[phase, BLK, t], sib, z).start()
        order = list(range(1, X)) + [0]

        @pl.when(z + 1 < R)
        def _():
            for n in order:
                remote(last, at(t, 0, W), snd.at[phase, DOWN], rcv.at[phase, TOP, t], same(n), z + 1).start()

        @pl.when(z > 0)
        def _():
            for n in order:
                remote(first, at(t, W + RP, W), snd.at[phase, UP], rcv.at[phase, BOT, t], same(n), z - 1).start()

    def forward(phase, at, which, src):
        sem = (0, UP, DOWN)[which]
        block = at(src, *spans[which])
        return remote(block, block, snd.at[phase, sem], rcv.at[phase, which, src], sib, z)

    def relay(phase, at, which, sources):
        for n in sources:
            c = forward(phase, at, which, same(n))
            c.wait_recv()
            c.start()

    def relay_rims(phase, at, sources):
        @pl.when(z > 0)
        def _():
            relay(phase, at, TOP, sources)

        @pl.when(z + 1 < R)
        def _():
            relay(phase, at, BOT, sources)

    def sibling_wait(phase, at, which):
        for n in range(X):
            forward(phase, at, which, other(n)).wait_recv()

    def gather_sent(phase, at, span_at):
        def done(block, sem):
            remote(block, block, snd.at[phase, sem], rcv.at[phase, BLK, t], sib, z).wait_send()

        done(span_at(T - 1, W, RP), 0)

        @pl.when(z + 1 < R)
        def _():
            done(span_at(T, 0, W), DOWN)

        @pl.when(z > 0)
        def _():
            done(span_at(T, 0, W), UP)

    def put_columns(f, offset, value):
        count = value.shape[0]
        active = value * (0.5 * jnp.tanh(0.5 * value) + 0.5)
        col = lax.rem(lax.broadcasted_iota(jnp.int32, (count, C), 0), W)
        before = jnp.where(col == 0, 0.0, pltpu.roll(active, 1, 0))
        after = jnp.where(col == W - 1, 0.0, pltpu.roll(active, count - 1, 0))
        cols[f, pl.ds(offset, count), 0:C] = before.astype(BF16)
        cols[f, pl.ds(offset, count), C : 2 * C] = active.astype(BF16)
        cols[f, pl.ds(offset, count), 2 * C : 3 * C] = after.astype(BF16)

    def conv(weights, taps):
        def stacked(parts):
            return parts[0] if len(parts) == 1 else jnp.concatenate(parts, axis=1)

        window = stacked([cols[:, j * W : j * W + RP, :].reshape(T * RP, 3 * C) for j in taps])
        both = stacked([weights[j, 0:2].reshape(2 * LANES, 3 * C) for j in taps])
        pair = lax.dot_general(window, both, NT, preferred_element_type=F32)
        if T <= 2:
            return pair, None
        last = stacked([weights[j, 2] for j in taps])
        return pair, lax.dot_general(window[: (T - 2) * RP], last, NT, preferred_element_type=F32)

    def both_parts(weights):
        return conv(weights, (0, 1, 2))

    def conv_frames(pair, single):
        results = []
        for f in range(T):
            value = pair[f * RP : (f + 1) * RP, :LANES]
            if f >= 1:
                value = value + pair[(f - 1) * RP : f * RP, LANES:]
            if f >= 2:
                value = value + single[(f - 2) * RP : (f - 1) * RP]
            results.append(value)
        return results

    zero_row = jnp.zeros((W, 3 * C), BF16)

    at1 = lambda src, offset, count: xin.at[src, pl.ds(offset, count), :]
    many1 = lambda count, offset, size: xin.at[pl.ds(0, count), pl.ds(offset, size), :]
    each(N - 1, lambda n: stat_copy(0, st1, n).start())
    gather_start(0, feat, feat.at[pl.ds(0, W), :], feat.at[pl.ds(RP - W, W), :], at1)
    xin[t, W : W + RP, :] = feat[...]
    lane1 = iota2((LANES, C), 0)
    spread1[...] = ones_where((lax.rem(lane1, GROUPS) == iota2((LANES, C), 1) // per) & (lane1 < 2 * GROUPS))
    stat_all(0, st1).wait_recv()

    gain1, shift1 = flat(g1), flat(s1)
    merged = jnp.concatenate(
        [merge_compact([st1[f * R + r] for r in range(R)], entries) for f in range(T)], axis=0)
    low = iota2((T, LANES), 1) < GROUPS
    wide = group_sum(
        jnp.concatenate([jnp.where(low, merged, 0.0), jnp.where(low, 0.0, merged)], axis=0), spread1[...])
    for f in range(T):
        norms[f] = jnp.concatenate([wide[f : f + 1], wide[T + f : T + f + 1] * gain1], axis=0)

    def norm1(f):
        return norms[f, 0:1, :], norms[f, 1:2, :]

    def fill1(f, offset, count):
        mean, scale = norm1(f)
        value = (xin[f, pl.ds(offset, count), :].astype(F32) - mean) * scale + shift1
        put_columns(f, offset, value)

    fill1(t, W, RP)
    relay(0, at1, BLK, range(1, X))
    for n in range(1, X):
        fill1(same(n), W, RP)
    relay_rims(0, at1, (0,))
    relay_rims(0, at1, range(1, X))
    sibling_wait(0, at1, BLK)
    for n in range(X):
        fill1(other(n), W, RP)

    taps_loaded(w1, 9)

    @pl.when(z > 0)
    def _():
        sibling_wait(0, at1, TOP)
        for f in range(T):
            fill1(f, 0, W)

    @pl.when(z == 0)
    def _():
        for f in range(T):
            cols[f, 0:W, :] = zero_row

    @pl.when(z + 1 < R)
    def _():
        sibling_wait(0, at1, BOT)
        for f in range(T):
            fill1(f, W + RP, W)

    @pl.when(z + 1 == R)
    def _():
        for f in range(T):
            cols[f, W + RP : EXT, :] = zero_row

    bias1 = padded(b1)
    acc = both_parts(w1)
    outs = [(v + bias1).astype(BF16).astype(F32) for v in conv_frames(*acc)]
    member_out = membership(LANES, per)
    if packed2:
        lane = lanes_of(RP)
        for f in range(T - 1):
            moved = pltpu.roll(outs[T - 1], 96 - 32 * f, 1)
            y1[t, f, W : W + RP, :] = jnp.where(lane >= 96, moved, outs[f]).astype(BF16)
    else:
        for f in range(T):
            y1[t, f, W : W + RP, :] = outs[f].astype(BF16)

    at2 = lambda src, offset, count: y1.at[src, :, pl.ds(offset, count), :]
    many2 = lambda count, offset, size: y1.at[pl.ds(0, count), :, pl.ds(offset, size), :]
    gather_start(1, at2(t, W, RP), at2(t, W, W), at2(t, RP, W), at2)
    mean, square = block_stats(outs, member_out, entries)
    held = OUT // per
    lane2 = iota2((LANES, LANES), 1)
    first = ones_where(iota2((LANES, LANES), 0) == per * lax.rem(lane2, held))
    both = group_sum(jnp.concatenate([mean, square], axis=0), first)
    chosen = iota2((2 * T, LANES), 1) // held == iota2((2 * T, LANES), 0)
    st2[me] = jnp.sum(jnp.where(chosen, both, 0.0), axis=0, keepdims=True)
    each(N - 1, lambda n: stat_copy(1, st2, n).start())

    pick = jnp.where(
        (lax.broadcasted_iota(jnp.int32, (C, LANES), 0)
         == t * OUT + lax.broadcasted_iota(jnp.int32, (C, LANES), 1))
        & (lax.broadcasted_iota(jnp.int32, (C, LANES), 1) < OUT), 1.0, 0.0).astype(BF16)
    own = jnp.dot(xin[:, W : W + RP, :].reshape(T * RP, C), pick, preferred_element_type=F32)
    pltpu.make_async_copy(aw, aw, lsem.at[11]).wait()
    mix[0] = (lax.dot_general(aw[0], aw[1], NT, preferred_element_type=F32) * C ** (-0.5)).astype(BF16)
    mix[1] = jnp.dot(aw[2], aw[3], preferred_element_type=F32).astype(BF16)

    for s in range(T):
        lane3, column = iota2((LANES, C), 0), iota2((LANES, C), 1)
        spread2[s * LANES : (s + 1) * LANES, :] = ones_where(
            (column // OUT == s) & (lax.rem(lane3, held) == lax.rem(column, OUT) // per))
    relay_rims(1, at2, (0,))
    relay(1, at2, BLK, range(1, X))
    relay_rims(1, at2, range(1, X))
    stat_all(1, st2).wait_recv()
    gain2, shift2 = flat(g2), flat(s2)
    holds = iota2((2 * T, LANES), 1) // held == iota2((2 * T, LANES), 0)
    merged = jnp.concatenate(
        [jnp.where(holds, merge_compact([st2[s * R + r] for r in range(R)], entries), 0.0) for s in range(T)], axis=1)
    wide = group_sum(merged, spread2[...])
    mean2, scale2 = wide[:T], wide[T:] * gain2

    def joined(blocks):
        return jnp.concatenate([b[:, :OUT] for b in blocks], axis=1)

    def conv_out(s, f, offset, count):
        if not packed2 or f < T - 1:
            return y1[s, f, offset : offset + count, :].astype(F32)
        lane = lanes_of(count)
        value = None
        for j in range(3):
            moved = pltpu.roll(y1[s, j, offset : offset + count, :].astype(F32), 32 + 32 * j, 1)
            value = moved if value is None else jnp.where(lane >= 32 * j, moved, value)
        return value

    def fill2(f, offset, count):
        raw = joined([conv_out(s, f, offset, count) for s in range(T)])
        value = (raw - mean2[f : f + 1]) * scale2[f : f + 1] + shift2
        put_columns(f, offset, value)

    sibling_wait(1, at2, BLK)
    for f in range(T):
        fill2(f, W, RP)
    taps_loaded(w2, 10)

    @pl.when(z > 0)
    def _():
        sibling_wait(1, at2, TOP)
        for f in range(T):
            fill2(f, 0, W)

    @pl.when(z + 1 < R)
    def _():
        sibling_wait(1, at2, BOT)
        for f in range(T):
            fill2(f, W + RP, W)

    bias2 = padded(b2)
    acc = both_parts(w2)
    for f, v in enumerate(conv_frames(*acc)):
        rounded = (v + bias2).astype(BF16).astype(F32)
        value = own[f * RP : (f + 1) * RP] + rounded
        hs[f] = (pack_rows(value) if packed3 else value).astype(BF16)

    def place(zz, tt):
        return hfull.at[zz * T + tt]

    def group(zz, count):
        return hfull.at[pl.ds(zz * T, count)]

    def hidden_start(pt, pz):
        remote(hs.at[pt], place(z, t), hid_s.at[0], hid_r.at[z], pt, pz).start()

    if R <= 4:
        for d in range(R - 1, 0, -1):
            for there in (z + d, z - d):
                @pl.when((there >= 0) & (there < R))
                def _():
                    for n in range(T):
                        hidden_start(lax.rem(t + n, T), there)
        for n in range(1, T):
            hidden_start(lax.rem(t + n, T), z)
    else:
        each(N - 1, lambda n: hidden_start(*peer(n + 1)))
    hfull[z * T + t] = hs[t]

    stat_all(0, st1).wait_send()
    gather_sent(0, at1, many1)
    stat_all(1, st2).wait_send()
    gather_sent(1, at2, many2)

    def arrived(zz, count):
        block = group(zz, count)
        remote(block, block, hid_s.at[0], hid_r.at[zz], lax.rem(t + 1, T), z).wait_recv()

    def take(zz):
        pieces = [place(zz, s)[...].astype(F32) for s in range(T)]
        value = joined([unpack_rows(p) for p in pieces] if packed3 else pieces)
        mean = jnp.sum(value, axis=0, keepdims=True) * (1.0 / RP)
        d = value - mean
        hid[pl.ds(pl.multiple_of(zz * RP, 16), RP), :] = value.astype(BF16)
        st3[zz] = jnp.concatenate([mean, jnp.sum(d * d, axis=0, keepdims=True)], axis=0)

    def arrival(zz):
        @pl.when(zz == z)
        def _():
            arrived(zz, T - 1)

        @pl.when(zz != z)
        def _():
            arrived(zz, T)

    def collect(n):
        zz = lax.rem(z + n, R)
        arrival(zz)
        take(zz)

    if R == 4:
        arrived(z, T - 1)
        take(z)
        for here, order in ((0, (1, 2, 3)), (1, (2, 0, 3)), (2, (1, 3, 0)), (3, (2, 1, 0))):
            @pl.when(z == here)
            def _():
                for zz in order:
                    arrived(zz, T)
                    take(zz)
    else:
        each(R, collect)

    means = [st3[r, 0:1, :] for r in range(R)]
    mean = group_sum(functools.reduce(lambda a, b: a + b, means), member) / (per * R)
    spread = functools.reduce(lambda a, b: a + b, [st3[r, 1:2, :] for r in range(R)])
    for m in means:
        d = m - mean
        spread = spread + RP * (d * d)
    var = group_sum(spread, member) / (entries * R)
    scale3 = lax.rsqrt(var + EPS) * flat(g3)
    shift3 = flat(s3)

    def normalise(r):
        part = pl.ds(pl.multiple_of(r * RP, 16), RP)
        normed[part, :] = ((hid[part, :].astype(F32) - mean) * scale3 + shift3).astype(BF16)

    each(R, normalise)
    mine = pl.ds(pl.multiple_of(z * RP, 16), RP)
    queries = jnp.dot(normed[mine, :], mix[0], preferred_element_type=F32).astype(BF16)
    scores = lax.dot_general(queries, normed[...], NT, preferred_element_type=F32)
    peak = jnp.max(scores, axis=1, keepdims=True)
    weights = jnp.exp(scores - peak)
    total = jnp.sum(weights, axis=1, keepdims=True)
    summed = jnp.dot(weights.astype(BF16), normed[...], preferred_element_type=F32)
    attended = (summed / total).astype(BF16)
    hidden = hid[mine, :].astype(F32)
    out[...] = (hidden + jnp.dot(attended, mix[1], preferred_element_type=F32)).astype(BF16)

    most = hfull.at[pl.ds(0, N - 1)]
    remote(most, most, hid_s.at[0], hid_r.at[z], sib, z).wait_send()


def solution(mesh):
    T, R = mesh.shape["tm"], mesh.shape["rows"]

    def per_device(features, g1, s1, k1, b1, g2, s2, k2, b2, g3, s3, wq, wk, wv, wo):
        _, rows, W, C = features.shape
        OUT = k1.shape[0]
        RP, EXT, N = rows * W, (rows + 2) * W, T * R
        taps = lambda k: jnp.transpose(k, (1, 2, 3, 0, 4))
        piece = 72 if OUT == 96 and RP == 96 else RP
        vmem = pl.BlockSpec(memory_space=pltpu.VMEM)
        hbm = pl.BlockSpec(memory_space=pltpu.HBM)
        dma = pltpu.SemaphoreType.DMA
        result = pl.pallas_call(
            functools.partial(kernel, T, R, W, rows, C, OUT),
            out_shape=pltpu.VMEM((RP, C), BF16),
            in_specs=[hbm] * 15,
            out_specs=vmem,
            scratch_shapes=[pltpu.VMEM((RP, C), BF16)] + [pltpu.VMEM((C,), F32)] * 6
            + [pltpu.VMEM((OUT,), F32)] * 2 + [
                pltpu.VMEM((T, EXT, C), BF16),
                pltpu.VMEM((T, 3 if T == 4 and OUT == 96 else T, EXT, LANES), BF16),
                pltpu.VMEM((T, EXT, 3 * C), BF16),
                pltpu.VMEM((3, 3, LANES, 3 * C), BF16),
                pltpu.VMEM((3, 3, LANES, 3 * C), BF16),
                pltpu.VMEM((4, C, C), BF16),
                pltpu.VMEM((N, 1, LANES), F32),
                pltpu.VMEM((N, 1, LANES), F32),
                pltpu.VMEM((R, 2, C), F32),
                pltpu.VMEM((T, piece, LANES), BF16),
                pltpu.VMEM((N, piece, LANES), BF16),
                pltpu.VMEM((R * RP, C), BF16),
                pltpu.VMEM((R * RP, C), BF16),
                pltpu.VMEM((2, C, C), BF16),
                pltpu.VMEM((LANES, C), BF16),
                pltpu.VMEM((T * LANES, C), BF16),
                pltpu.VMEM((T, 2, C), F32),
                dma((12,)), dma((2, 3)), dma((2, 3, T)), dma((2,)), dma((2,)), dma((1,)), dma((R,)),
            ],
            compiler_params=pltpu.CompilerParams(
                collective_id=0, has_side_effects=True, vmem_limit_bytes=62 * 1024 * 1024),
        )(features.reshape(RP, C), g1, s1, taps(k1), b1, g2, s2,
          taps(k2), b2, g3, s3, wq, wk, wv, wo)
        return result.reshape(features.shape)

    in_specs = (
        P(("clips", "tm"), "rows", None, None), P(), P(),
        P("tm", None, None, None, None), P("tm"), P(), P(),
        P("tm", None, None, None, None), P("tm"), P(), P(), P(), P(), P(), P(),
    )
    return jax.shard_map(
        per_device, mesh=mesh, in_specs=in_specs,
        out_specs=P(("clips", "tm"), "rows", None, None), check_vma=False)
```

```python
import functools

import jax
import jax.numpy as jnp
from jax import lax
from jax.experimental import pallas as pl
from jax.experimental.pallas import tpu as pltpu
from jax.sharding import PartitionSpec as P

GROUPS = 32
EPS = 1e-06
LANES = 128
MESH = pl.DeviceIdType.MESH
F32 = jnp.float32
BF16 = jnp.bfloat16
NT = (((1,), (1,)), ((), ()))


def flat(ref):
    return ref[...].reshape(1, ref.shape[0])


def padded(ref):
    row = flat(ref)
    rest = LANES - ref.shape[0]
    return jnp.concatenate([row, jnp.zeros((1, rest), F32)], axis=1) if rest else row


def each(count, body):
    if count <= 16:
        for n in range(count):
            body(n)
    else:
        lax.fori_loop(0, count, lambda n, c: (body(n), c)[1], 0)


def membership(size, per_group):
    a = lax.broadcasted_iota(jnp.int32, (size, size), 0) // per_group
    b = lax.broadcasted_iota(jnp.int32, (size, size), 1) // per_group
    return jnp.where(a == b, 1.0, 0.0).astype(BF16)


def group_sum(rows, member):
    hi = rows.astype(BF16).astype(F32)
    rest = rows - hi
    mid = rest.astype(BF16).astype(F32)
    low = rest - mid
    count = rows.shape[0]
    terms = jnp.concatenate([hi, mid, low], axis=0).astype(BF16)
    out = jnp.dot(terms, member, preferred_element_type=F32)
    return out[:count] + out[count : 2 * count] + out[2 * count :]


def block_stats(blocks, member, entries):
    sums = jnp.concatenate([jnp.sum(b, axis=0, keepdims=True) for b in blocks], axis=0)
    means = group_sum(sums, member) / entries
    squares = []
    for n, b in enumerate(blocks):
        d = b - means[n : n + 1]
        squares.append(jnp.sum(d * d, axis=0, keepdims=True))
    return means, group_sum(jnp.concatenate(squares, axis=0), member)


def merge_stats(means, squares, entries):
    count = len(means)
    mean = functools.reduce(lambda a, b: a + b, means) / count
    total = functools.reduce(lambda a, b: a + b, squares)
    for m in means:
        d = m - mean
        total = total + entries * (d * d)
    return mean, lax.rsqrt(total / (count * entries) + EPS)


def lanes_of(count):
    return lax.broadcasted_iota(jnp.int32, (count, LANES), 1)


def pack_rows(v):
    tail = v[72:96]
    lane = lanes_of(24)
    parts = []
    for j in range(3):
        moved = pltpu.roll(tail, 96 - 32 * j, 1)
        parts.append(jnp.where(lane >= 96, moved, v[24 * j : 24 * j + 24]))
    return jnp.concatenate(parts, axis=0)


def unpack_rows(p):
    lane = lanes_of(24)
    tail = jnp.zeros((24, LANES), F32)
    for j in range(3):
        moved = pltpu.roll(p[24 * j : 24 * j + 24], 32 + 32 * j, 1)
        tail = jnp.where((lane >= 32 * j) & (lane < 32 * j + 32), moved, tail)
    return jnp.concatenate([p, tail], axis=0)


def iota2(shape, axis):
    return lax.broadcasted_iota(jnp.int32, shape, axis)


def ones_where(mask):
    return jnp.where(mask, 1.0, 0.0).astype(BF16)


def merge_compact(blocks, entries):
    count = len(blocks)
    mean = functools.reduce(lambda a, b: a + b, blocks) / count
    total = functools.reduce(lambda a, b: a + b, blocks)
    for b in blocks:
        d = pltpu.roll(b - mean, GROUPS, 1)
        total = total + entries * (d * d)
    inv = lax.rsqrt(total / (count * entries) + EPS)
    return jnp.where(iota2(mean.shape, 1) < GROUPS, mean, inv)


def kernel(T, R, W, rows, C, OUT,
           feath, g1h, s1h, w1h, b1h, g2h, s2h, w2h, b2h, g3h, s3h, wqh, wkh, wvh, woh,
           out,
           feat, g1, s1, g2, s2, g3, s3, b1, b2, xin, y1, cols, w1, w2, aw, st1, st2, st3, hs, hfull, hid, normed, mix, spread1, spread2, norms,
           lsem, snd, rcv, st_s, st_r, hid_s, hid_r):
    t = lax.axis_index("tm")
    z = lax.axis_index("rows")
    me = t * R + z
    N = T * R
    RP = rows * W
    EXT = (rows + 2) * W
    per = C // GROUPS
    entries = RP * per
    packed2 = y1.shape[1] < T
    packed3 = hs.shape[1] < RP

    def peer(p):
        other = lax.rem(me + p, N)
        return other // R, lax.rem(other, R)

    barrier = pltpu.get_barrier_semaphore()

    def greet(n):
        pt, pz = peer(n + 1)
        pl.semaphore_signal(barrier, inc=1, device_id={"tm": pt, "rows": pz}, device_id_type=MESH)

    small = [
        pltpu.make_async_copy(src, dst, lsem.at[n])
        for n, (src, dst) in enumerate((
            (feath, feat), (g1h, g1), (s1h, s1), (g2h, g2), (s2h, s2), (g3h, g3), (s3h, s3),
            (b1h, b1), (b2h, b2)))
    ]
    small[0].start()
    each(N - 1, greet)
    for load in small[1:]:
        load.start()

    def load_taps(src, dst, n):
        for i in range(3):
            for k in range(3):
                pltpu.make_async_copy(
                    src.at[i, :, k], dst.at[:, 2 - i, pl.ds(0, OUT), pl.ds(k * C, C)], lsem.at[n]).start()

    def taps_loaded(dst, n):
        whole = dst.at[:, :, pl.ds(0, OUT), :]
        pltpu.make_async_copy(whole, whole, lsem.at[n]).wait()

    load_taps(w1h, w1, 9)
    for n, src in enumerate((wqh, wkh, wvh, woh)):
        pltpu.make_async_copy(src, aw.at[n], lsem.at[11]).start()
    load_taps(w2h, w2, 10)

    def remote(src, dst, ssem, rsem, pt, pz):
        return pltpu.make_async_remote_copy(
            src_ref=src, dst_ref=dst, send_sem=ssem, recv_sem=rsem,
            device_id={"tm": pt, "rows": pz}, device_id_type=MESH)

    small[0].wait()
    x = feat[...].astype(F32)
    member = membership(C, per)
    mean, square = block_stats([x], member, entries)
    first = ones_where(iota2((C, LANES), 0) == per * lax.rem(iota2((C, LANES), 1), GROUPS))
    both = group_sum(jnp.concatenate([mean, square], axis=0), first)
    st1[me] = jnp.where(iota2((1, LANES), 1) < GROUPS, both[0:1], both[1:2])
    for load in small[1:]:
        load.wait()
    if OUT < LANES:
        w1[:, :, OUT:, :] = jnp.zeros((3, 3, LANES - OUT, 3 * C), BF16)
        w2[:, :, OUT:, :] = jnp.zeros((3, 3, LANES - OUT, 3 * C), BF16)

    pl.semaphore_wait(barrier, N - 1)

    def stat_copy(phase, ref, n):
        pt, pz = peer(n + 1)
        return remote(ref.at[me], ref.at[me], st_s.at[phase], st_r.at[phase], pt, pz)

    def stat_all(phase, ref):
        most = ref.at[pl.ds(0, N - 1)]
        return remote(most, most, st_s.at[phase], st_r.at[phase], lax.rem(t + 1, T), z)

    core = lax.rem(t, 2)
    sib = t + 1 - 2 * core
    X = T // 2
    chip = t // 2

    def same(n):
        return 2 * lax.rem(chip + n, X) + core

    def other(n):
        return 2 * lax.rem(chip + n, X) + 1 - core

    BLK, TOP, BOT = 0, 1, 2
    DOWN, UP = 1, 2
    spans = ((W, RP), (0, W), (W + RP, W))

    def gather_start(phase, body, first, last, at):
        for n in range(1, X):
            remote(body, at(t, W, RP), snd.at[phase, 0], rcv.at[phase, BLK, t], same(n), z).start()
        remote(body, at(t, W, RP), snd.at[phase, 0], rcv.at[phase, BLK, t], sib, z).start()
        order = list(range(1, X)) + [0]

        @pl.when(z + 1 < R)
        def _():
            for n in order:
                remote(last, at(t, 0, W), snd.at[phase, DOWN], rcv.at[phase, TOP, t], same(n), z + 1).start()

        @pl.when(z > 0)
        def _():
            for n in order:
                remote(first, at(t, W + RP, W), snd.at[phase, UP], rcv.at[phase, BOT, t], same(n), z - 1).start()

    def forward(phase, at, which, src):
        sem = (0, UP, DOWN)[which]
        block = at(src, *spans[which])
        return remote(block, block, snd.at[phase, sem], rcv.at[phase, which, src], sib, z)

    def relay(phase, at, which, sources):
        for n in sources:
            c = forward(phase, at, which, same(n))
            c.wait_recv()
            c.start()

    def relay_rims(phase, at, sources):
        @pl.when(z > 0)
        def _():
            relay(phase, at, TOP, sources)

        @pl.when(z + 1 < R)
        def _():
            relay(phase, at, BOT, sources)

    def sibling_wait(phase, at, which):
        for n in range(X):
            forward(phase, at, which, other(n)).wait_recv()

    def gather_sent(phase, at, span_at):
        def done(block, sem):
            remote(block, block, snd.at[phase, sem], rcv.at[phase, BLK, t], sib, z).wait_send()

        done(span_at(T - 1, W, RP), 0)

        @pl.when(z + 1 < R)
        def _():
            done(span_at(T, 0, W), DOWN)

        @pl.when(z > 0)
        def _():
            done(span_at(T, 0, W), UP)

    def put_columns(f, offset, value):
        count = value.shape[0]
        active = value * (0.5 * jnp.tanh(0.5 * value) + 0.5)
        col = lax.rem(lax.broadcasted_iota(jnp.int32, (count, C), 0), W)
        before = jnp.where(col == 0, 0.0, pltpu.roll(active, 1, 0))
        after = jnp.where(col == W - 1, 0.0, pltpu.roll(active, count - 1, 0))
        cols[f, pl.ds(offset, count), 0:C] = before.astype(BF16)
        cols[f, pl.ds(offset, count), C : 2 * C] = active.astype(BF16)
        cols[f, pl.ds(offset, count), 2 * C : 3 * C] = after.astype(BF16)

    def conv(weights, taps):
        def stacked(parts):
            return parts[0] if len(parts) == 1 else jnp.concatenate(parts, axis=1)

        window = stacked([cols[:, j * W : j * W + RP, :].reshape(T * RP, 3 * C) for j in taps])
        both = stacked([weights[j, 0:2].reshape(2 * LANES, 3 * C) for j in taps])
        pair = lax.dot_general(window, both, NT, preferred_element_type=F32)
        if T <= 2:
            return pair, None
        last = stacked([weights[j, 2] for j in taps])
        return pair, lax.dot_general(window[: (T - 2) * RP], last, NT, preferred_element_type=F32)

    def both_parts(weights):
        return conv(weights, (0, 1, 2))

    def conv_frames(pair, single):
        results = []
        for f in range(T):
            value = pair[f * RP : (f + 1) * RP, :LANES]
            if f >= 1:
                value = value + pair[(f - 1) * RP : f * RP, LANES:]
            if f >= 2:
                value = value + single[(f - 2) * RP : (f - 1) * RP]
            results.append(value)
        return results

    zero_row = jnp.zeros((W, 3 * C), BF16)

    at1 = lambda src, offset, count: xin.at[src, pl.ds(offset, count), :]
    many1 = lambda count, offset, size: xin.at[pl.ds(0, count), pl.ds(offset, size), :]
    each(N - 1, lambda n: stat_copy(0, st1, n).start())
    gather_start(0, feat, feat.at[pl.ds(0, W), :], feat.at[pl.ds(RP - W, W), :], at1)
    xin[t, W : W + RP, :] = feat[...]
    lane1 = iota2((LANES, C), 0)
    spread1[...] = ones_where((lax.rem(lane1, GROUPS) == iota2((LANES, C), 1) // per) & (lane1 < 2 * GROUPS))
    relay(0, at1, BLK, range(1, X))
    relay_rims(0, at1, (0,))
    relay_rims(0, at1, range(1, X))
    stat_all(0, st1).wait_recv()

    gain1, shift1 = flat(g1), flat(s1)
    merged = jnp.concatenate(
        [merge_compact([st1[f * R + r] for r in range(R)], entries) for f in range(T)], axis=0)
    low = iota2((T, LANES), 1) < GROUPS
    wide = group_sum(
        jnp.concatenate([jnp.where(low, merged, 0.0), jnp.where(low, 0.0, merged)], axis=0), spread1[...])
    for f in range(T):
        norms[f] = jnp.concatenate([wide[f : f + 1], wide[T + f : T + f + 1] * gain1], axis=0)

    def norm1(f):
        return norms[f, 0:1, :], norms[f, 1:2, :]

    def fill1(f, offset, count):
        mean, scale = norm1(f)
        value = (xin[f, pl.ds(offset, count), :].astype(F32) - mean) * scale + shift1
        put_columns(f, offset, value)

    fill1(t, W, RP)
    for n in range(1, X):
        fill1(same(n), W, RP)
    sibling_wait(0, at1, BLK)
    for n in range(X):
        fill1(other(n), W, RP)

    taps_loaded(w1, 9)

    @pl.when(z > 0)
    def _():
        sibling_wait(0, at1, TOP)
        for f in range(T):
            fill1(f, 0, W)

    @pl.when(z == 0)
    def _():
        for f in range(T):
            cols[f, 0:W, :] = zero_row

    @pl.when(z + 1 < R)
    def _():
        sibling_wait(0, at1, BOT)
        for f in range(T):
            fill1(f, W + RP, W)

    @pl.when(z + 1 == R)
    def _():
        for f in range(T):
            cols[f, W + RP : EXT, :] = zero_row

    bias1 = padded(b1)
    acc = both_parts(w1)
    outs = [(v + bias1).astype(BF16).astype(F32) for v in conv_frames(*acc)]
    member_out = membership(LANES, per)
    if packed2:
        lane = lanes_of(RP)
        for f in range(T - 1):
            moved = pltpu.roll(outs[T - 1], 96 - 32 * f, 1)
            y1[t, f, W : W + RP, :] = jnp.where(lane >= 96, moved, outs[f]).astype(BF16)
    else:
        for f in range(T):
            y1[t, f, W : W + RP, :] = outs[f].astype(BF16)

    at2 = lambda src, offset, count: y1.at[src, :, pl.ds(offset, count), :]
    many2 = lambda count, offset, size: y1.at[pl.ds(0, count), :, pl.ds(offset, size), :]
    gather_start(1, at2(t, W, RP), at2(t, W, W), at2(t, RP, W), at2)
    mean, square = block_stats(outs, member_out, entries)
    held = OUT // per
    lane2 = iota2((LANES, LANES), 1)
    first = ones_where(iota2((LANES, LANES), 0) == per * lax.rem(lane2, held))
    both = group_sum(jnp.concatenate([mean, square], axis=0), first)
    chosen = iota2((2 * T, LANES), 1) // held == iota2((2 * T, LANES), 0)
    st2[me] = jnp.sum(jnp.where(chosen, both, 0.0), axis=0, keepdims=True)
    each(N - 1, lambda n: stat_copy(1, st2, n).start())

    pick = jnp.where(
        (lax.broadcasted_iota(jnp.int32, (C, LANES), 0)
         == t * OUT + lax.broadcasted_iota(jnp.int32, (C, LANES), 1))
        & (lax.broadcasted_iota(jnp.int32, (C, LANES), 1) < OUT), 1.0, 0.0).astype(BF16)
    own = jnp.dot(xin[:, W : W + RP, :].reshape(T * RP, C), pick, preferred_element_type=F32)
    pltpu.make_async_copy(aw, aw, lsem.at[11]).wait()
    mix[0] = (lax.dot_general(aw[0], aw[1], NT, preferred_element_type=F32) * C ** (-0.5)).astype(BF16)
    mix[1] = jnp.dot(aw[2], aw[3], preferred_element_type=F32).astype(BF16)

    for s in range(T):
        lane3, column = iota2((LANES, C), 0), iota2((LANES, C), 1)
        spread2[s * LANES : (s + 1) * LANES, :] = ones_where(
            (column // OUT == s) & (lax.rem(lane3, held) == lax.rem(column, OUT) // per))
    relay_rims(1, at2, (0,))
    relay(1, at2, BLK, range(1, X))
    relay_rims(1, at2, range(1, X))
    stat_all(1, st2).wait_recv()
    gain2, shift2 = flat(g2), flat(s2)
    holds = iota2((2 * T, LANES), 1) // held == iota2((2 * T, LANES), 0)
    merged = jnp.concatenate(
        [jnp.where(holds, merge_compact([st2[s * R + r] for r in range(R)], entries), 0.0) for s in range(T)], axis=1)
    wide = group_sum(merged, spread2[...])
    mean2, scale2 = wide[:T], wide[T:] * gain2

    def joined(blocks):
        return jnp.concatenate([b[:, :OUT] for b in blocks], axis=1)

    def conv_out(s, f, offset, count):
        if not packed2 or f < T - 1:
            return y1[s, f, offset : offset + count, :].astype(F32)
        lane = lanes_of(count)
        value = None
        for j in range(3):
            moved = pltpu.roll(y1[s, j, offset : offset + count, :].astype(F32), 32 + 32 * j, 1)
            value = moved if value is None else jnp.where(lane >= 32 * j, moved, value)
        return value

    def fill2(f, offset, count):
        raw = joined([conv_out(s, f, offset, count) for s in range(T)])
        value = (raw - mean2[f : f + 1]) * scale2[f : f + 1] + shift2
        put_columns(f, offset, value)

    sibling_wait(1, at2, BLK)
    for f in range(T):
        fill2(f, W, RP)
    taps_loaded(w2, 10)

    @pl.when(z > 0)
    def _():
        sibling_wait(1, at2, TOP)
        for f in range(T):
            fill2(f, 0, W)

    @pl.when(z + 1 < R)
    def _():
        sibling_wait(1, at2, BOT)
        for f in range(T):
            fill2(f, W + RP, W)

    bias2 = padded(b2)
    acc = both_parts(w2)
    for f, v in enumerate(conv_frames(*acc)):
        rounded = (v + bias2).astype(BF16).astype(F32)
        value = own[f * RP : (f + 1) * RP] + rounded
        hs[f] = (pack_rows(value) if packed3 else value).astype(BF16)

    def place(zz, tt):
        return hfull.at[zz * T + tt]

    def group(zz, count):
        return hfull.at[pl.ds(zz * T, count)]

    def hidden_start(pt, pz):
        remote(hs.at[pt], place(z, t), hid_s.at[0], hid_r.at[z], pt, pz).start()

    if R == 4:
        for here, order in ((0, (2, 1)), (1, (0, 2, 3)), (2, (0, 1, 3)), (3, (0, 2))):
            @pl.when(z == here)
            def _():
                for there in order:
                    for n in range(T):
                        hidden_start(lax.rem(t + n, T), there)
        for n in range(1, T):
            hidden_start(lax.rem(t + n, T), z)
    else:
        each(N - 1, lambda n: hidden_start(*peer(n + 1)))
    hfull[z * T + t] = hs[t]

    stat_all(0, st1).wait_send()
    gather_sent(0, at1, many1)
    stat_all(1, st2).wait_send()
    gather_sent(1, at2, many2)

    def arrived(zz, count):
        block = group(zz, count)
        remote(block, block, hid_s.at[0], hid_r.at[zz], lax.rem(t + 1, T), z).wait_recv()

    def block_of(zz):
        pieces = [place(zz, s)[...].astype(F32) for s in range(T)]
        return joined([unpack_rows(p) for p in pieces] if packed3 else pieces)

    def take(zz, centre, value=None):
        value = block_of(zz) if value is None else value
        d = value - centre
        hid[pl.ds(pl.multiple_of(zz * RP, 16), RP), :] = value.astype(BF16)
        st3[...] += jnp.concatenate(
            [jnp.sum(d, axis=0, keepdims=True), jnp.sum(d * d, axis=0, keepdims=True)], axis=0)

    def forwarded(zz):
        return remote(group(zz, T), group(zz, T), hid_s.at[1 + zz // 3], hid_r.at[zz], t, 3 - zz * 2 // 3)

    if R == 4:
        for here, source in ((2, 3), (2, 0)):
            @pl.when(z == here)
            def _():
                arrived(source, T)
                forwarded(source).start()

    st3[...] = jnp.zeros((2, C), F32)
    arrived(z, T - 1)
    mine_now = block_of(z)
    centre = group_sum(jnp.sum(mine_now, axis=0, keepdims=True), member) / entries
    take(z, centre, mine_now)
    if R == 4:
        for here, order in ((0, (1, 2, 3)), (1, (3, 0, 2)), (2, (0, 3, 1)), (3, (2, 1, 0))):
            @pl.when(z == here)
            def _():
                for zz in order:
                    if (here, zz) not in ((2, 0), (2, 3)):
                        arrived(zz, T)
                    take(zz, centre)
    else:
        def collect(n):
            zz = lax.rem(z + n + 1, R)
            arrived(zz, T)
            take(zz, centre)

        each(R - 1, collect)

    moments = group_sum(st3[...], member) / (entries * R)
    mean = centre + moments[0:1]
    var = moments[1:2] - moments[0:1] * moments[0:1]
    scale3 = lax.rsqrt(var + EPS) * flat(g3)
    shift3 = flat(s3)

    def normalise(r):
        part = pl.ds(pl.multiple_of(r * RP, 16), RP)
        normed[part, :] = ((hid[part, :].astype(F32) - mean) * scale3 + shift3).astype(BF16)

    each(R, normalise)
    mine = pl.ds(pl.multiple_of(z * RP, 16), RP)
    queries = jnp.dot(normed[mine, :], mix[0], preferred_element_type=F32).astype(BF16)
    scores = lax.dot_general(queries, normed[...], NT, preferred_element_type=F32)
    peak = jnp.max(scores, axis=1, keepdims=True)
    weights = jnp.exp(scores - peak)
    total = jnp.sum(weights, axis=1, keepdims=True)
    summed = jnp.dot(weights.astype(BF16), normed[...], preferred_element_type=F32)
    projected = jnp.dot(summed.astype(BF16), mix[1], preferred_element_type=F32)
    out[...] = (hid[mine, :].astype(F32) + projected / total).astype(BF16)

    def hidden_sent(count):
        most = hfull.at[pl.ds(0, count)]
        remote(most, most, hid_s.at[0], hid_r.at[z], sib, z).wait_send()

    if R == 4:
        for here, source in ((2, 3), (2, 0)):
            @pl.when(z == here)
            def _():
                forwarded(source).wait_send()

        @pl.when((z == 0) | (z == 3))
        def _():
            hidden_sent(N - 1 - T)

        @pl.when((z == 1) | (z == 2))
        def _():
            hidden_sent(N - 1)
    else:
        hidden_sent(N - 1)


def solution(mesh):
    T, R = mesh.shape["tm"], mesh.shape["rows"]

    def per_device(features, g1, s1, k1, b1, g2, s2, k2, b2, g3, s3, wq, wk, wv, wo):
        _, rows, W, C = features.shape
        OUT = k1.shape[0]
        RP, EXT, N = rows * W, (rows + 2) * W, T * R
        taps = lambda k: jnp.transpose(k, (1, 2, 3, 0, 4))
        piece = 72 if OUT == 96 and RP == 96 else RP
        vmem = pl.BlockSpec(memory_space=pltpu.VMEM)
        hbm = pl.BlockSpec(memory_space=pltpu.HBM)
        dma = pltpu.SemaphoreType.DMA
        result = pl.pallas_call(
            functools.partial(kernel, T, R, W, rows, C, OUT),
            out_shape=pltpu.VMEM((RP, C), BF16),
            in_specs=[hbm] * 15,
            out_specs=vmem,
            scratch_shapes=[pltpu.VMEM((RP, C), BF16)] + [pltpu.VMEM((C,), F32)] * 6
            + [pltpu.VMEM((OUT,), F32)] * 2 + [
                pltpu.VMEM((T, EXT, C), BF16),
                pltpu.VMEM((T, 3 if T == 4 and OUT == 96 else T, EXT, LANES), BF16),
                pltpu.VMEM((T, EXT, 3 * C), BF16),
                pltpu.VMEM((3, 3, LANES, 3 * C), BF16),
                pltpu.VMEM((3, 3, LANES, 3 * C), BF16),
                pltpu.VMEM((4, C, C), BF16),
                pltpu.VMEM((N, 1, LANES), F32),
                pltpu.VMEM((N, 1, LANES), F32),
                pltpu.VMEM((2, C), F32),
                pltpu.VMEM((T, piece, LANES), BF16),
                pltpu.VMEM((N, piece, LANES), BF16),
                pltpu.VMEM((R * RP, C), BF16),
                pltpu.VMEM((R * RP, C), BF16),
                pltpu.VMEM((2, C, C), BF16),
                pltpu.VMEM((LANES, C), BF16),
                pltpu.VMEM((T * LANES, C), BF16),
                pltpu.VMEM((T, 2, C), F32),
                dma((12,)), dma((2, 3)), dma((2, 3, T)), dma((2,)), dma((2,)), dma((3,)), dma((R,)),
            ],
            compiler_params=pltpu.CompilerParams(
                collective_id=0, has_side_effects=True, vmem_limit_bytes=62 * 1024 * 1024),
        )(features.reshape(RP, C), g1, s1, taps(k1), b1, g2, s2,
          taps(k2), b2, g3, s3, wq, wk, wv, wo)
        return result.reshape(features.shape)

    in_specs = (
        P(("clips", "tm"), "rows", None, None), P(), P(),
        P("tm", None, None, None, None), P("tm"), P(), P(),
        P("tm", None, None, None, None), P("tm"), P(), P(), P(), P(), P(), P(),
    )
    return jax.shard_map(
        per_device, mesh=mesh, in_specs=in_specs,
        out_specs=P(("clips", "tm"), "rows", None, None), check_vma=False)
```

```python
import functools

import jax
import jax.numpy as jnp
from jax import lax
from jax.experimental import pallas as pl
from jax.experimental.pallas import tpu as pltpu
from jax.sharding import PartitionSpec as P

GROUPS = 32
EPS = 1e-06
LANES = 128
MESH = pl.DeviceIdType.MESH
F32 = jnp.float32
BF16 = jnp.bfloat16
NT = (((1,), (1,)), ((), ()))


def flat(ref):
    return ref[...].reshape(1, ref.shape[0])


def padded(ref):
    row = flat(ref)
    rest = LANES - ref.shape[0]
    return jnp.concatenate([row, jnp.zeros((1, rest), F32)], axis=1) if rest else row


def each(count, body):
    if count <= 16:
        for n in range(count):
            body(n)
    else:
        lax.fori_loop(0, count, lambda n, c: (body(n), c)[1], 0)


def membership(size, per_group):
    a = lax.broadcasted_iota(jnp.int32, (size, size), 0) // per_group
    b = lax.broadcasted_iota(jnp.int32, (size, size), 1) // per_group
    return jnp.where(a == b, 1.0, 0.0).astype(BF16)


def group_sum(rows, member):
    hi = rows.astype(BF16).astype(F32)
    rest = rows - hi
    mid = rest.astype(BF16).astype(F32)
    low = rest - mid
    count = rows.shape[0]
    terms = jnp.concatenate([hi, mid, low], axis=0).astype(BF16)
    out = jnp.dot(terms, member, preferred_element_type=F32)
    return out[:count] + out[count : 2 * count] + out[2 * count :]


def block_stats(blocks, member, entries):
    sums = jnp.concatenate([jnp.sum(b, axis=0, keepdims=True) for b in blocks], axis=0)
    means = group_sum(sums, member) / entries
    squares = []
    for n, b in enumerate(blocks):
        d = b - means[n : n + 1]
        squares.append(jnp.sum(d * d, axis=0, keepdims=True))
    return means, group_sum(jnp.concatenate(squares, axis=0), member)


def merge_stats(means, squares, entries):
    count = len(means)
    mean = functools.reduce(lambda a, b: a + b, means) / count
    total = functools.reduce(lambda a, b: a + b, squares)
    for m in means:
        d = m - mean
        total = total + entries * (d * d)
    return mean, lax.rsqrt(total / (count * entries) + EPS)


def lanes_of(count):
    return lax.broadcasted_iota(jnp.int32, (count, LANES), 1)


def pack_rows(v):
    tail = v[72:96]
    lane = lanes_of(24)
    parts = []
    for j in range(3):
        moved = pltpu.roll(tail, 96 - 32 * j, 1)
        parts.append(jnp.where(lane >= 96, moved, v[24 * j : 24 * j + 24]))
    return jnp.concatenate(parts, axis=0)


def unpack_rows(p):
    lane = lanes_of(24)
    tail = jnp.zeros((24, LANES), F32)
    for j in range(3):
        moved = pltpu.roll(p[24 * j : 24 * j + 24], 32 + 32 * j, 1)
        tail = jnp.where((lane >= 32 * j) & (lane < 32 * j + 32), moved, tail)
    return jnp.concatenate([p, tail], axis=0)


def iota2(shape, axis):
    return lax.broadcasted_iota(jnp.int32, shape, axis)


def ones_where(mask):
    return jnp.where(mask, 1.0, 0.0).astype(BF16)


def merge_compact(blocks, entries):
    count = len(blocks)
    mean = functools.reduce(lambda a, b: a + b, blocks) / count
    total = functools.reduce(lambda a, b: a + b, blocks)
    for b in blocks:
        d = pltpu.roll(b - mean, GROUPS, 1)
        total = total + entries * (d * d)
    inv = lax.rsqrt(total / (count * entries) + EPS)
    return jnp.where(iota2(mean.shape, 1) < GROUPS, mean, inv)


def kernel(T, R, W, rows, C, OUT,
           feath, g1h, s1h, w1h, b1h, g2h, s2h, w2h, b2h, g3h, s3h, wqh, wkh, wvh, woh,
           out,
           feat, g1, s1, g2, s2, g3, s3, b1, b2, xin, y1, cols, w1, w2, aw, st1, st2, st3, hs, hfull, hid, normed, mix, spread1, spread2, norms,
           lsem, snd, rcv, st_s, st_r, hid_s, hid_r):
    t = lax.axis_index("tm")
    z = lax.axis_index("rows")
    me = t * R + z
    N = T * R
    RP = rows * W
    EXT = (rows + 2) * W
    per = C // GROUPS
    entries = RP * per
    packed2 = y1.shape[1] < T
    packed3 = hs.shape[1] < RP

    def peer(p):
        other = lax.rem(me + p, N)
        return other // R, lax.rem(other, R)

    barrier = pltpu.get_barrier_semaphore()

    def greet(n):
        pt, pz = peer(n + 1)
        pl.semaphore_signal(barrier, inc=1, device_id={"tm": pt, "rows": pz}, device_id_type=MESH)

    small = [
        pltpu.make_async_copy(src, dst, lsem.at[n])
        for n, (src, dst) in enumerate((
            (feath, feat), (g1h, g1), (s1h, s1), (g2h, g2), (s2h, s2), (g3h, g3), (s3h, s3),
            (b1h, b1), (b2h, b2)))
    ]
    small[0].start()
    chained = R == 4

    def at_row(here):
        return pl.when(z == here)

    def row_greet(here):
        rows_of = [here] + [zz for zz in range(R) if zz > here or zz == here - 1 or (here, zz) == (2, 0)]
        for zz in rows_of:
            for n in range(1 if zz == here else 0, T):
                pl.semaphore_signal(
                    barrier, inc=1, device_id={"tm": lax.rem(t + n, T), "rows": zz}, device_id_type=MESH)

    if chained:
        for here in range(R):
            at_row(here)(functools.partial(row_greet, here))
    else:
        each(N - 1, greet)
    for load in small[1:]:
        load.start()

    def load_taps(src, dst, n):
        for i in range(3):
            for k in range(3):
                pltpu.make_async_copy(
                    src.at[i, :, k], dst.at[:, 2 - i, pl.ds(0, OUT), pl.ds(k * C, C)], lsem.at[n]).start()

    def taps_loaded(dst, n):
        whole = dst.at[:, :, pl.ds(0, OUT), :]
        pltpu.make_async_copy(whole, whole, lsem.at[n]).wait()

    load_taps(w1h, w1, 9)
    for n, src in enumerate((wqh, wkh, wvh, woh)):
        pltpu.make_async_copy(src, aw.at[n], lsem.at[11]).start()
    load_taps(w2h, w2, 10)

    def remote(src, dst, ssem, rsem, pt, pz):
        return pltpu.make_async_remote_copy(
            src_ref=src, dst_ref=dst, send_sem=ssem, recv_sem=rsem,
            device_id={"tm": pt, "rows": pz}, device_id_type=MESH)

    small[0].wait()
    x = feat[...].astype(F32)
    member = membership(C, per)
    mean, square = block_stats([x], member, entries)
    first = ones_where(iota2((C, LANES), 0) == per * lax.rem(iota2((C, LANES), 1), GROUPS))
    both = group_sum(jnp.concatenate([mean, square], axis=0), first)
    st1[me] = jnp.where(iota2((1, LANES), 1) < GROUPS, both[0:1], both[1:2])
    for load in small[1:]:
        load.wait()
    if OUT < LANES:
        w1[:, :, OUT:, :] = jnp.zeros((3, 3, LANES - OUT, 3 * C), BF16)
        w2[:, :, OUT:, :] = jnp.zeros((3, 3, LANES - OUT, 3 * C), BF16)

    if chained:
        pl.semaphore_wait(barrier, 3 * T - 1 + T * (z // 2))
    else:
        pl.semaphore_wait(barrier, N - 1)

    def stat_copy(phase, ref, n):
        pt, pz = peer(n + 1)
        return remote(ref.at[me], ref.at[me], st_s.at[phase], st_r.at[phase], pt, pz)

    def stat_all(phase, ref):
        most = ref.at[pl.ds(0, N - 1)]
        return remote(most, most, st_s.at[phase], st_r.at[phase], lax.rem(t + 1, T), z)

    core = lax.rem(t, 2)
    sib = t + 1 - 2 * core
    X = T // 2
    chip = t // 2

    def same(n):
        return 2 * lax.rem(chip + n, X) + core

    def other(n):
        return 2 * lax.rem(chip + n, X) + 1 - core

    BLK, TOP, BOT = 0, 1, 2
    DOWN, UP = 1, 2
    spans = ((W, RP), (0, W), (W + RP, W))

    def gather_start(phase, body, first, last, at):
        for n in range(1, X):
            remote(body, at(t, W, RP), snd.at[phase, 0], rcv.at[phase, BLK, t], same(n), z).start()
        remote(body, at(t, W, RP), snd.at[phase, 0], rcv.at[phase, BLK, t], sib, z).start()
        order = list(range(1, X)) + [0]

        @pl.when(z + 1 < R)
        def _():
            for n in order:
                remote(last, at(t, 0, W), snd.at[phase, DOWN], rcv.at[phase, TOP, t], same(n), z + 1).start()

        @pl.when(z > 0)
        def _():
            for n in order:
                remote(first, at(t, W + RP, W), snd.at[phase, UP], rcv.at[phase, BOT, t], same(n), z - 1).start()

    def forward(phase, at, which, src):
        sem = (0, UP, DOWN)[which]
        block = at(src, *spans[which])
        return remote(block, block, snd.at[phase, sem], rcv.at[phase, which, src], sib, z)

    def relay(phase, at, which, sources):
        for n in sources:
            c = forward(phase, at, which, same(n))
            c.wait_recv()
            c.start()

    def relay_rims(phase, at, sources):
        @pl.when(z > 0)
        def _():
            relay(phase, at, TOP, sources)

        @pl.when(z + 1 < R)
        def _():
            relay(phase, at, BOT, sources)

    def sibling_wait(phase, at, which):
        for n in range(X):
            forward(phase, at, which, other(n)).wait_recv()

    def gather_sent(phase, at, span_at):
        def done(block, sem):
            remote(block, block, snd.at[phase, sem], rcv.at[phase, BLK, t], sib, z).wait_send()

        done(span_at(T - 1, W, RP), 0)

        @pl.when(z + 1 < R)
        def _():
            done(span_at(T, 0, W), DOWN)

        @pl.when(z > 0)
        def _():
            done(span_at(T, 0, W), UP)

    def put_columns(f, offset, value):
        count = value.shape[0]
        active = value * (0.5 * jnp.tanh(0.5 * value) + 0.5)
        col = lax.rem(lax.broadcasted_iota(jnp.int32, (count, C), 0), W)
        before = jnp.where(col == 0, 0.0, pltpu.roll(active, 1, 0))
        after = jnp.where(col == W - 1, 0.0, pltpu.roll(active, count - 1, 0))
        cols[f, pl.ds(offset, count), 0:C] = before.astype(BF16)
        cols[f, pl.ds(offset, count), C : 2 * C] = active.astype(BF16)
        cols[f, pl.ds(offset, count), 2 * C : 3 * C] = after.astype(BF16)

    def conv(weights, taps):
        def stacked(parts):
            return parts[0] if len(parts) == 1 else jnp.concatenate(parts, axis=1)

        window = stacked([cols[:, j * W : j * W + RP, :].reshape(T * RP, 3 * C) for j in taps])
        both = stacked([weights[j, 0:2].reshape(2 * LANES, 3 * C) for j in taps])
        pair = lax.dot_general(window, both, NT, preferred_element_type=F32)
        if T <= 2:
            return pair, None
        last = stacked([weights[j, 2] for j in taps])
        return pair, lax.dot_general(window[: (T - 2) * RP], last, NT, preferred_element_type=F32)

    def both_parts(weights):
        return conv(weights, (0, 1, 2))

    def conv_frames(pair, single):
        results = []
        for f in range(T):
            value = pair[f * RP : (f + 1) * RP, :LANES]
            if f >= 1:
                value = value + pair[(f - 1) * RP : f * RP, LANES:]
            if f >= 2:
                value = value + single[(f - 2) * RP : (f - 1) * RP]
            results.append(value)
        return results

    zero_row = jnp.zeros((W, 3 * C), BF16)

    at1 = lambda src, offset, count: xin.at[src, pl.ds(offset, count), :]
    many1 = lambda count, offset, size: xin.at[pl.ds(0, count), pl.ds(offset, size), :]
    targets_of = ((0, 1, 2), (1, 0, 2), (2, 0, 1), (3, 0, 1, 2))

    def row_sends(here):
        for zz in targets_of[here]:
            for n in range(1 if zz == here else 0, T):
                sem = 2 if n == 0 and here < 2 and zz == 2 else 0
                remote(st1.at[me], st1.at[me], st_s.at[0], st_r.at[sem], lax.rem(t + n, T), zz).start()

    def column(count):
        return st1.at[pl.ds(t * R, count)]

    def pass_up(here):
        remote(column(2), column(2), st_s.at[2], st_r.at[2], sib, z).wait_recv()
        for n in range(T):
            remote(column(3), column(3), st_s.at[2], st_r.at[0], lax.rem(t + n, T), 3).start()

    def row_stats(here):
        most = st1.at[pl.ds(0, N - 3 if here == 2 else N - 1)]
        remote(most, most, st_s.at[0], st_r.at[0], sib, z).wait_recv()

    def row_sent(here):
        most = st1.at[pl.ds(0, T * len(targets_of[here]) - 1)]
        remote(most, most, st_s.at[0], st_r.at[0], sib, z).wait_send()
        if here == 2:
            most = st1.at[pl.ds(0, 3 * T)]
            remote(most, most, st_s.at[2], st_r.at[0], sib, z).wait_send()

    def by_row(body, which):
        for here in which:
            at_row(here)(functools.partial(body, here))

    if chained:
        by_row(row_sends, range(R))
    else:
        each(N - 1, lambda n: stat_copy(0, st1, n).start())
    gather_start(0, feat, feat.at[pl.ds(0, W), :], feat.at[pl.ds(RP - W, W), :], at1)
    xin[t, W : W + RP, :] = feat[...]
    lane1 = iota2((LANES, C), 0)
    spread1[...] = ones_where((lax.rem(lane1, GROUPS) == iota2((LANES, C), 1) // per) & (lane1 < 2 * GROUPS))
    if chained:
        by_row(pass_up, (2,))
    relay(0, at1, BLK, range(1, X))
    relay_rims(0, at1, (0,))
    relay_rims(0, at1, range(1, X))
    if chained:
        by_row(row_stats, range(R))
    else:
        stat_all(0, st1).wait_recv()

    gain1, shift1 = flat(g1), flat(s1)
    merged = jnp.concatenate(
        [merge_compact([st1[f * R + r] for r in range(R)], entries) for f in range(T)], axis=0)
    low = iota2((T, LANES), 1) < GROUPS
    wide = group_sum(
        jnp.concatenate([jnp.where(low, merged, 0.0), jnp.where(low, 0.0, merged)], axis=0), spread1[...])
    for f in range(T):
        norms[f] = jnp.concatenate([wide[f : f + 1], wide[T + f : T + f + 1] * gain1], axis=0)

    def norm1(f):
        return norms[f, 0:1, :], norms[f, 1:2, :]

    def fill1(f, offset, count):
        mean, scale = norm1(f)
        value = (xin[f, pl.ds(offset, count), :].astype(F32) - mean) * scale + shift1
        put_columns(f, offset, value)

    fill1(t, W, RP)
    for n in range(1, X):
        fill1(same(n), W, RP)
    sibling_wait(0, at1, BLK)
    for n in range(X):
        fill1(other(n), W, RP)

    taps_loaded(w1, 9)

    @pl.when(z > 0)
    def _():
        sibling_wait(0, at1, TOP)
        for f in range(T):
            fill1(f, 0, W)

    @pl.when(z == 0)
    def _():
        for f in range(T):
            cols[f, 0:W, :] = zero_row

    @pl.when(z + 1 < R)
    def _():
        sibling_wait(0, at1, BOT)
        for f in range(T):
            fill1(f, W + RP, W)

    @pl.when(z + 1 == R)
    def _():
        for f in range(T):
            cols[f, W + RP : EXT, :] = zero_row

    bias1 = padded(b1)
    acc = both_parts(w1)
    outs = [(v + bias1).astype(BF16).astype(F32) for v in conv_frames(*acc)]
    member_out = membership(LANES, per)
    if packed2:
        lane = lanes_of(RP)
        for f in range(T - 1):
            moved = pltpu.roll(outs[T - 1], 96 - 32 * f, 1)
            y1[t, f, W : W + RP, :] = jnp.where(lane >= 96, moved, outs[f]).astype(BF16)
    else:
        for f in range(T):
            y1[t, f, W : W + RP, :] = outs[f].astype(BF16)

    at2 = lambda src, offset, count: y1.at[src, :, pl.ds(offset, count), :]
    many2 = lambda count, offset, size: y1.at[pl.ds(0, count), :, pl.ds(offset, size), :]
    gather_start(1, at2(t, W, RP), at2(t, W, W), at2(t, RP, W), at2)
    mean, square = block_stats(outs, member_out, entries)
    held = OUT // per
    lane2 = iota2((LANES, LANES), 1)
    first = ones_where(iota2((LANES, LANES), 0) == per * lax.rem(lane2, held))
    both = group_sum(jnp.concatenate([mean, square], axis=0), first)
    chosen = iota2((2 * T, LANES), 1) // held == iota2((2 * T, LANES), 0)
    st2[me] = jnp.sum(jnp.where(chosen, both, 0.0), axis=0, keepdims=True)
    each(N - 1, lambda n: stat_copy(1, st2, n).start())

    pick = jnp.where(
        (lax.broadcasted_iota(jnp.int32, (C, LANES), 0)
         == t * OUT + lax.broadcasted_iota(jnp.int32, (C, LANES), 1))
        & (lax.broadcasted_iota(jnp.int32, (C, LANES), 1) < OUT), 1.0, 0.0).astype(BF16)
    own = jnp.dot(xin[:, W : W + RP, :].reshape(T * RP, C), pick, preferred_element_type=F32)
    pltpu.make_async_copy(aw, aw, lsem.at[11]).wait()
    mix[0] = (lax.dot_general(aw[0], aw[1], NT, preferred_element_type=F32) * C ** (-0.5)).astype(BF16)
    mix[1] = jnp.dot(aw[2], aw[3], preferred_element_type=F32).astype(BF16)

    for s in range(T):
        lane3, column = iota2((LANES, C), 0), iota2((LANES, C), 1)
        spread2[s * LANES : (s + 1) * LANES, :] = ones_where(
            (column // OUT == s) & (lax.rem(lane3, held) == lax.rem(column, OUT) // per))
    relay_rims(1, at2, (0,))
    relay(1, at2, BLK, range(1, X))
    relay_rims(1, at2, range(1, X))
    stat_all(1, st2).wait_recv()
    gain2, shift2 = flat(g2), flat(s2)
    holds = iota2((2 * T, LANES), 1) // held == iota2((2 * T, LANES), 0)
    merged = jnp.concatenate(
        [jnp.where(holds, merge_compact([st2[s * R + r] for r in range(R)], entries), 0.0) for s in range(T)], axis=1)
    wide = group_sum(merged, spread2[...])
    mean2, scale2 = wide[:T], wide[T:] * gain2

    def joined(blocks):
        return jnp.concatenate([b[:, :OUT] for b in blocks], axis=1)

    def conv_out(s, f, offset, count):
        if not packed2 or f < T - 1:
            return y1[s, f, offset : offset + count, :].astype(F32)
        lane = lanes_of(count)
        value = None
        for j in range(3):
            moved = pltpu.roll(y1[s, j, offset : offset + count, :].astype(F32), 32 + 32 * j, 1)
            value = moved if value is None else jnp.where(lane >= 32 * j, moved, value)
        return value

    def fill2(f, offset, count):
        raw = joined([conv_out(s, f, offset, count) for s in range(T)])
        value = (raw - mean2[f : f + 1]) * scale2[f : f + 1] + shift2
        put_columns(f, offset, value)

    sibling_wait(1, at2, BLK)
    for f in range(T):
        fill2(f, W, RP)
    taps_loaded(w2, 10)

    @pl.when(z > 0)
    def _():
        sibling_wait(1, at2, TOP)
        for f in range(T):
            fill2(f, 0, W)

    @pl.when(z + 1 < R)
    def _():
        sibling_wait(1, at2, BOT)
        for f in range(T):
            fill2(f, W + RP, W)

    bias2 = padded(b2)
    acc = both_parts(w2)
    for f, v in enumerate(conv_frames(*acc)):
        rounded = (v + bias2).astype(BF16).astype(F32)
        value = own[f * RP : (f + 1) * RP] + rounded
        hs[f] = (pack_rows(value) if packed3 else value).astype(BF16)

    def place(zz, tt):
        return hfull.at[zz * T + tt]

    def group(zz, count):
        return hfull.at[pl.ds(zz * T, count)]

    def hidden_start(pt, pz):
        remote(hs.at[pt], place(z, t), hid_s.at[0], hid_r.at[z], pt, pz).start()

    if R == 4:
        for here, order in ((0, (2, 1)), (1, (0, 2, 3)), (2, (0, 1, 3)), (3, (0, 2))):
            @pl.when(z == here)
            def _():
                for there in order:
                    for n in range(T):
                        hidden_start(lax.rem(t + n, T), there)
        for n in range(1, T):
            hidden_start(lax.rem(t + n, T), z)
    else:
        each(N - 1, lambda n: hidden_start(*peer(n + 1)))
    hfull[z * T + t] = hs[t]

    if chained:
        by_row(row_sent, range(R))
    else:
        stat_all(0, st1).wait_send()
    gather_sent(0, at1, many1)
    stat_all(1, st2).wait_send()
    gather_sent(1, at2, many2)

    def arrived(zz, count):
        block = group(zz, count)
        remote(block, block, hid_s.at[0], hid_r.at[zz], lax.rem(t + 1, T), z).wait_recv()

    def block_of(zz):
        pieces = [place(zz, s)[...].astype(F32) for s in range(T)]
        return joined([unpack_rows(p) for p in pieces] if packed3 else pieces)

    def take(zz, centre, value=None):
        value = block_of(zz) if value is None else value
        d = value - centre
        hid[pl.ds(pl.multiple_of(zz * RP, 16), RP), :] = value.astype(BF16)
        st3[...] += jnp.concatenate(
            [jnp.sum(d, axis=0, keepdims=True), jnp.sum(d * d, axis=0, keepdims=True)], axis=0)

    def forwarded(zz):
        return remote(group(zz, T), group(zz, T), hid_s.at[1 + zz // 3], hid_r.at[zz], t, 3 - zz * 2 // 3)

    if R == 4:
        for here, source in ((2, 3), (2, 0)):
            @pl.when(z == here)
            def _():
                arrived(source, T)
                forwarded(source).start()

    st3[...] = jnp.zeros((2, C), F32)
    arrived(z, T - 1)
    mine_now = block_of(z)
    centre = group_sum(jnp.sum(mine_now, axis=0, keepdims=True), member) / entries
    take(z, centre, mine_now)
    if R == 4:
        for here, order in ((0, (1, 2, 3)), (1, (3, 0, 2)), (2, (0, 3, 1)), (3, (2, 1, 0))):
            @pl.when(z == here)
            def _():
                for zz in order:
                    if (here, zz) not in ((2, 0), (2, 3)):
                        arrived(zz, T)
                    take(zz, centre)
    else:
        def collect(n):
            zz = lax.rem(z + n + 1, R)
            arrived(zz, T)
            take(zz, centre)

        each(R - 1, collect)

    moments = group_sum(st3[...], member) / (entries * R)
    mean = centre + moments[0:1]
    var = moments[1:2] - moments[0:1] * moments[0:1]
    scale3 = lax.rsqrt(var + EPS) * flat(g3)
    shift3 = flat(s3)

    def normalise(r):
        part = pl.ds(pl.multiple_of(r * RP, 16), RP)
        normed[part, :] = ((hid[part, :].astype(F32) - mean) * scale3 + shift3).astype(BF16)

    each(R, normalise)
    mine = pl.ds(pl.multiple_of(z * RP, 16), RP)
    queries = jnp.dot(normed[mine, :], mix[0], preferred_element_type=F32).astype(BF16)
    scores = lax.dot_general(queries, normed[...], NT, preferred_element_type=F32)
    peak = jnp.max(scores, axis=1, keepdims=True)
    weights = jnp.exp(scores - peak)
    total = jnp.sum(weights, axis=1, keepdims=True)
    summed = jnp.dot(weights.astype(BF16), normed[...], preferred_element_type=F32)
    projected = jnp.dot(summed.astype(BF16), mix[1], preferred_element_type=F32)
    out[...] = (hid[mine, :].astype(F32) + projected / total).astype(BF16)

    def hidden_sent(count):
        most = hfull.at[pl.ds(0, count)]
        remote(most, most, hid_s.at[0], hid_r.at[z], sib, z).wait_send()

    if R == 4:
        for here, source in ((2, 3), (2, 0)):
            @pl.when(z == here)
            def _():
                forwarded(source).wait_send()

        @pl.when((z == 0) | (z == 3))
        def _():
            hidden_sent(N - 1 - T)

        @pl.when((z == 1) | (z == 2))
        def _():
            hidden_sent(N - 1)
    else:
        hidden_sent(N - 1)


def solution(mesh):
    T, R = mesh.shape["tm"], mesh.shape["rows"]

    def per_device(features, g1, s1, k1, b1, g2, s2, k2, b2, g3, s3, wq, wk, wv, wo):
        _, rows, W, C = features.shape
        OUT = k1.shape[0]
        RP, EXT, N = rows * W, (rows + 2) * W, T * R
        taps = lambda k: jnp.transpose(k, (1, 2, 3, 0, 4))
        piece = 72 if OUT == 96 and RP == 96 else RP
        vmem = pl.BlockSpec(memory_space=pltpu.VMEM)
        hbm = pl.BlockSpec(memory_space=pltpu.HBM)
        dma = pltpu.SemaphoreType.DMA
        result = pl.pallas_call(
            functools.partial(kernel, T, R, W, rows, C, OUT),
            out_shape=pltpu.VMEM((RP, C), BF16),
            in_specs=[hbm] * 15,
            out_specs=vmem,
            scratch_shapes=[pltpu.VMEM((RP, C), BF16)] + [pltpu.VMEM((C,), F32)] * 6
            + [pltpu.VMEM((OUT,), F32)] * 2 + [
                pltpu.VMEM((T, EXT, C), BF16),
                pltpu.VMEM((T, 3 if T == 4 and OUT == 96 else T, EXT, LANES), BF16),
                pltpu.VMEM((T, EXT, 3 * C), BF16),
                pltpu.VMEM((3, 3, LANES, 3 * C), BF16),
                pltpu.VMEM((3, 3, LANES, 3 * C), BF16),
                pltpu.VMEM((4, C, C), BF16),
                pltpu.VMEM((N, 1, LANES), F32),
                pltpu.VMEM((N, 1, LANES), F32),
                pltpu.VMEM((2, C), F32),
                pltpu.VMEM((T, piece, LANES), BF16),
                pltpu.VMEM((N, piece, LANES), BF16),
                pltpu.VMEM((R * RP, C), BF16),
                pltpu.VMEM((R * RP, C), BF16),
                pltpu.VMEM((2, C, C), BF16),
                pltpu.VMEM((LANES, C), BF16),
                pltpu.VMEM((T * LANES, C), BF16),
                pltpu.VMEM((T, 2, C), F32),
                dma((12,)), dma((2, 3)), dma((2, 3, T)), dma((3,)), dma((3,)), dma((3,)), dma((R,)),
            ],
            compiler_params=pltpu.CompilerParams(
                collective_id=0, has_side_effects=True, vmem_limit_bytes=62 * 1024 * 1024),
        )(features.reshape(RP, C), g1, s1, taps(k1), b1, g2, s2,
          taps(k2), b2, g3, s3, wq, wk, wv, wo)
        return result.reshape(features.shape)

    in_specs = (
        P(("clips", "tm"), "rows", None, None), P(), P(),
        P("tm", None, None, None, None), P("tm"), P(), P(),
        P("tm", None, None, None, None), P("tm"), P(), P(), P(), P(), P(), P(),
    )
    return jax.shard_map(
        per_device, mesh=mesh, in_specs=in_specs,
        out_specs=P(("clips", "tm"), "rows", None, None), check_vma=False)
```

```python
import functools

import jax
import jax.numpy as jnp
from jax import lax
from jax.experimental import pallas as pl
from jax.experimental.pallas import tpu as pltpu
from jax.sharding import PartitionSpec as P

GROUPS = 32
EPS = 1e-06
LANES = 128
MESH = pl.DeviceIdType.MESH
F32 = jnp.float32
BF16 = jnp.bfloat16
NT = (((1,), (1,)), ((), ()))


def flat(ref):
    return ref[...].reshape(1, ref.shape[0])


def padded(ref):
    row = flat(ref)
    rest = LANES - ref.shape[0]
    return jnp.concatenate([row, jnp.zeros((1, rest), F32)], axis=1) if rest else row


def each(count, body):
    if count <= 16:
        for n in range(count):
            body(n)
    else:
        lax.fori_loop(0, count, lambda n, c: (body(n), c)[1], 0)


def membership(size, per_group):
    a = lax.broadcasted_iota(jnp.int32, (size, size), 0) // per_group
    b = lax.broadcasted_iota(jnp.int32, (size, size), 1) // per_group
    return jnp.where(a == b, 1.0, 0.0).astype(BF16)


def group_sum(rows, member):
    hi = rows.astype(BF16).astype(F32)
    rest = rows - hi
    mid = rest.astype(BF16).astype(F32)
    low = rest - mid
    count = rows.shape[0]
    terms = jnp.concatenate([hi, mid, low], axis=0).astype(BF16)
    out = jnp.dot(terms, member, preferred_element_type=F32)
    return out[:count] + out[count : 2 * count] + out[2 * count :]


def block_stats(blocks, member, entries):
    sums = jnp.concatenate([jnp.sum(b, axis=0, keepdims=True) for b in blocks], axis=0)
    means = group_sum(sums, member) / entries
    squares = []
    for n, b in enumerate(blocks):
        d = b - means[n : n + 1]
        squares.append(jnp.sum(d * d, axis=0, keepdims=True))
    return means, group_sum(jnp.concatenate(squares, axis=0), member)


def merge_stats(means, squares, entries):
    count = len(means)
    mean = functools.reduce(lambda a, b: a + b, means) / count
    total = functools.reduce(lambda a, b: a + b, squares)
    for m in means:
        d = m - mean
        total = total + entries * (d * d)
    return mean, lax.rsqrt(total / (count * entries) + EPS)


def lanes_of(count):
    return lax.broadcasted_iota(jnp.int32, (count, LANES), 1)


def pack_rows(v):
    tail = v[72:96]
    lane = lanes_of(24)
    parts = []
    for j in range(3):
        moved = pltpu.roll(tail, 96 - 32 * j, 1)
        parts.append(jnp.where(lane >= 96, moved, v[24 * j : 24 * j + 24]))
    return jnp.concatenate(parts, axis=0)


def unpack_rows(p):
    lane = lanes_of(24)
    tail = jnp.zeros((24, LANES), F32)
    for j in range(3):
        moved = pltpu.roll(p[24 * j : 24 * j + 24], 32 + 32 * j, 1)
        tail = jnp.where((lane >= 32 * j) & (lane < 32 * j + 32), moved, tail)
    return jnp.concatenate([p, tail], axis=0)


def iota2(shape, axis):
    return lax.broadcasted_iota(jnp.int32, shape, axis)


def ones_where(mask):
    return jnp.where(mask, 1.0, 0.0).astype(BF16)


def merge_compact(blocks, entries):
    count = len(blocks)
    mean = functools.reduce(lambda a, b: a + b, blocks) / count
    total = functools.reduce(lambda a, b: a + b, blocks)
    for b in blocks:
        d = pltpu.roll(b - mean, GROUPS, 1)
        total = total + entries * (d * d)
    inv = lax.rsqrt(total / (count * entries) + EPS)
    return jnp.where(iota2(mean.shape, 1) < GROUPS, mean, inv)


def kernel(T, R, W, rows, C, OUT,
           feath, g1h, s1h, w1h, b1h, g2h, s2h, w2h, b2h, g3h, s3h, wqh, wkh, wvh, woh,
           out,
           feat, g1, s1, g2, s2, g3, s3, b1, b2, xin, y1, cols, w1, w2, aw, st1, st2, st3, hs, hfull, hid, normed, mix, spread1, spread2, norms,
           lsem, snd, rcv, st_r, hid_r):
    t = lax.axis_index("tm")
    z = lax.axis_index("rows")
    me = t * R + z
    N = T * R
    RP = rows * W
    EXT = (rows + 2) * W
    per = C // GROUPS
    entries = RP * per
    packed2 = y1.shape[1] < T
    packed3 = hs.shape[1] < RP

    def peer(p):
        other = lax.rem(me + p, N)
        return other // R, lax.rem(other, R)

    barrier = pltpu.get_barrier_semaphore()

    def greet(n):
        pt, pz = peer(n + 1)
        pl.semaphore_signal(barrier, inc=1, device_id={"tm": pt, "rows": pz}, device_id_type=MESH)

    small = [
        pltpu.make_async_copy(src, dst, lsem.at[n])
        for n, (src, dst) in enumerate((
            (feath, feat), (g1h, g1), (s1h, s1), (g2h, g2), (s2h, s2), (g3h, g3), (s3h, s3),
            (b1h, b1), (b2h, b2)))
    ]
    small[0].start()
    chained = R == 4

    def at_row(here):
        return pl.when(z == here)

    def row_greet(here):
        rows_of = [here] + [zz for zz in range(R) if zz > here or zz == here - 1 or (here, zz) == (2, 0)]
        for zz in rows_of:
            for n in range(1 if zz == here else 0, T):
                pl.semaphore_signal(
                    barrier, inc=1, device_id={"tm": lax.rem(t + n, T), "rows": zz}, device_id_type=MESH)

    if chained:
        for here in range(R):
            at_row(here)(functools.partial(row_greet, here))
    else:
        each(N - 1, greet)
    for load in small[1:]:
        load.start()

    def load_taps(src, dst, n):
        for i in range(3):
            for k in range(3):
                pltpu.make_async_copy(
                    src.at[i, :, k], dst.at[:, 2 - i, pl.ds(0, OUT), pl.ds(k * C, C)], lsem.at[n]).start()

    def taps_loaded(dst, n):
        whole = dst.at[:, :, pl.ds(0, OUT), :]
        pltpu.make_async_copy(whole, whole, lsem.at[n]).wait()

    load_taps(w1h, w1, 9)
    for n, src in enumerate((wqh, wkh, wvh, woh)):
        pltpu.make_async_copy(src, aw.at[n], lsem.at[11]).start()
    load_taps(w2h, w2, 10)

    def remote(src, dst, ssem, rsem, pt, pz):
        return pltpu.make_async_remote_copy(
            src_ref=src, dst_ref=dst, send_sem=ssem, recv_sem=rsem,
            device_id={"tm": pt, "rows": pz}, device_id_type=MESH)

    small[0].wait()
    x = feat[...].astype(F32)
    member = membership(C, per)
    mean, square = block_stats([x], member, entries)
    first = ones_where(iota2((C, LANES), 0) == per * lax.rem(iota2((C, LANES), 1), GROUPS))
    both = group_sum(jnp.concatenate([mean, square], axis=0), first)
    st1[me] = jnp.where(iota2((1, LANES), 1) < GROUPS, both[0:1], both[1:2])
    for load in small[1:]:
        load.wait()
    if OUT < LANES:
        w1[:, :, OUT:, :] = jnp.zeros((3, 3, LANES - OUT, 3 * C), BF16)
        w2[:, :, OUT:, :] = jnp.zeros((3, 3, LANES - OUT, 3 * C), BF16)

    if chained:
        pl.semaphore_wait(barrier, 3 * T - 1 + T * (z // 2))
    else:
        pl.semaphore_wait(barrier, N - 1)

    def stat_copy(phase, ref, n):
        pt, pz = peer(n + 1)
        return remote(ref.at[me], ref.at[me], lsem.at[4 + phase], st_r.at[phase], pt, pz)

    def stat_all(phase, ref):
        most = ref.at[pl.ds(0, N - 1)]
        return remote(most, most, lsem.at[4 + phase], st_r.at[phase], lax.rem(t + 1, T), z)

    core = lax.rem(t, 2)
    sib = t + 1 - 2 * core
    X = T // 2
    chip = t // 2

    def same(n):
        return 2 * lax.rem(chip + n, X) + core

    def other(n):
        return 2 * lax.rem(chip + n, X) + 1 - core

    BLK, TOP, BOT = 0, 1, 2
    DOWN, UP = 1, 2
    spans = ((W, RP), (0, W), (W + RP, W))

    def gather_start(phase, body, first, last, at):
        for n in range(1, X):
            remote(body, at(t, W, RP), snd.at[phase, 0], rcv.at[phase, BLK, t], same(n), z).start()
        remote(body, at(t, W, RP), snd.at[phase, 0], rcv.at[phase, BLK, t], sib, z).start()
        order = list(range(1, X)) + [0]

        @pl.when(z + 1 < R)
        def _():
            for n in order:
                remote(last, at(t, 0, W), snd.at[phase, DOWN], rcv.at[phase, TOP, t], same(n), z + 1).start()

        @pl.when(z > 0)
        def _():
            for n in order:
                remote(first, at(t, W + RP, W), snd.at[phase, UP], rcv.at[phase, BOT, t], same(n), z - 1).start()

    def forward(phase, at, which, src):
        sem = (0, UP, DOWN)[which]
        block = at(src, *spans[which])
        return remote(block, block, snd.at[phase, sem], rcv.at[phase, which, src], sib, z)

    def relay(phase, at, which, sources):
        for n in sources:
            c = forward(phase, at, which, same(n))
            c.wait_recv()
            c.start()

    def relay_rims(phase, at, sources):
        @pl.when(z > 0)
        def _():
            relay(phase, at, TOP, sources)

        @pl.when(z + 1 < R)
        def _():
            relay(phase, at, BOT, sources)

    def sibling_wait(phase, at, which):
        for n in range(X):
            forward(phase, at, which, other(n)).wait_recv()

    def gather_sent(phase, at, span_at):
        def done(block, sem):
            remote(block, block, snd.at[phase, sem], rcv.at[phase, BLK, t], sib, z).wait_send()

        done(span_at(T - 1, W, RP), 0)

        @pl.when(z + 1 < R)
        def _():
            done(span_at(T, 0, W), DOWN)

        @pl.when(z > 0)
        def _():
            done(span_at(T, 0, W), UP)

    def put_columns(f, offset, value):
        count = value.shape[0]
        active = value * (0.5 * jnp.tanh(0.5 * value) + 0.5)
        col = lax.rem(lax.broadcasted_iota(jnp.int32, (count, C), 0), W)
        before = jnp.where(col == 0, 0.0, pltpu.roll(active, 1, 0))
        after = jnp.where(col == W - 1, 0.0, pltpu.roll(active, count - 1, 0))
        cols[f, pl.ds(offset, count), 0:C] = before.astype(BF16)
        cols[f, pl.ds(offset, count), C : 2 * C] = active.astype(BF16)
        cols[f, pl.ds(offset, count), 2 * C : 3 * C] = after.astype(BF16)

    def conv(weights, taps):
        def stacked(parts):
            return parts[0] if len(parts) == 1 else jnp.concatenate(parts, axis=1)

        window = stacked([cols[:, j * W : j * W + RP, :].reshape(T * RP, 3 * C) for j in taps])
        both = stacked([weights[j, 0:2].reshape(2 * LANES, 3 * C) for j in taps])
        pair = lax.dot_general(window, both, NT, preferred_element_type=F32)
        if T <= 2:
            return pair, None
        last = stacked([weights[j, 2] for j in taps])
        return pair, lax.dot_general(window[: (T - 2) * RP], last, NT, preferred_element_type=F32)

    def both_parts(weights):
        return conv(weights, (0, 1, 2))

    def conv_frames(pair, single):
        results = []
        for f in range(T):
            value = pair[f * RP : (f + 1) * RP, :LANES]
            if f >= 1:
                value = value + pair[(f - 1) * RP : f * RP, LANES:]
            if f >= 2:
                value = value + single[(f - 2) * RP : (f - 1) * RP]
            results.append(value)
        return results

    zero_row = jnp.zeros((W, 3 * C), BF16)

    at1 = lambda src, offset, count: xin.at[src, pl.ds(offset, count), :]
    many1 = lambda count, offset, size: xin.at[pl.ds(0, count), pl.ds(offset, size), :]
    targets_of = ((0, 1, 2), (1, 0, 2), (2, 0, 1), (3, 0, 1, 2))

    def row_sends(here):
        for zz in targets_of[here]:
            for n in range(1 if zz == here else 0, T):
                sem = 2 if n == 0 and here < 2 and zz == 2 else 0
                remote(st1.at[me], st1.at[me], lsem.at[4], st_r.at[sem], lax.rem(t + n, T), zz).start()

    def column(count):
        return st1.at[pl.ds(t * R, count)]

    def pass_up(here):
        remote(column(2), column(2), lsem.at[6], st_r.at[2], sib, z).wait_recv()
        for n in range(T):
            remote(column(3), column(3), lsem.at[6], st_r.at[0], lax.rem(t + n, T), 3).start()

    def row_stats(here):
        most = st1.at[pl.ds(0, N - 3 if here == 2 else N - 1)]
        remote(most, most, lsem.at[4], st_r.at[0], sib, z).wait_recv()

    def row_sent(here):
        most = st1.at[pl.ds(0, T * len(targets_of[here]) - 1)]
        remote(most, most, lsem.at[4], st_r.at[0], sib, z).wait_send()
        if here == 2:
            most = st1.at[pl.ds(0, 3 * T)]
            remote(most, most, lsem.at[6], st_r.at[0], sib, z).wait_send()

    def by_row(body, which):
        for here in which:
            at_row(here)(functools.partial(body, here))

    if chained:
        by_row(row_sends, range(R))
    else:
        each(N - 1, lambda n: stat_copy(0, st1, n).start())
    gather_start(0, feat, feat.at[pl.ds(0, W), :], feat.at[pl.ds(RP - W, W), :], at1)
    xin[t, W : W + RP, :] = feat[...]
    lane1 = iota2((LANES, C), 0)
    spread1[...] = ones_where((lax.rem(lane1, GROUPS) == iota2((LANES, C), 1) // per) & (lane1 < 2 * GROUPS))
    if chained:
        by_row(pass_up, (2,))
    relay(0, at1, BLK, range(1, X))
    relay_rims(0, at1, (0,))
    relay_rims(0, at1, range(1, X))
    if chained:
        by_row(row_stats, range(R))
    else:
        stat_all(0, st1).wait_recv()

    gain1, shift1 = flat(g1), flat(s1)
    merged = jnp.concatenate(
        [merge_compact([st1[f * R + r] for r in range(R)], entries) for f in range(T)], axis=0)
    low = iota2((T, LANES), 1) < GROUPS
    wide = group_sum(
        jnp.concatenate([jnp.where(low, merged, 0.0), jnp.where(low, 0.0, merged)], axis=0), spread1[...])
    for f in range(T):
        norms[f] = jnp.concatenate([wide[f : f + 1], wide[T + f : T + f + 1] * gain1], axis=0)

    def norm1(f):
        return norms[f, 0:1, :], norms[f, 1:2, :]

    def fill1(f, offset, count):
        mean, scale = norm1(f)
        value = (xin[f, pl.ds(offset, count), :].astype(F32) - mean) * scale + shift1
        put_columns(f, offset, value)

    fill1(t, W, RP)
    for n in range(1, X):
        fill1(same(n), W, RP)
    sibling_wait(0, at1, BLK)
    for n in range(X):
        fill1(other(n), W, RP)

    taps_loaded(w1, 9)

    @pl.when(z > 0)
    def _():
        sibling_wait(0, at1, TOP)
        for f in range(T):
            fill1(f, 0, W)

    @pl.when(z == 0)
    def _():
        for f in range(T):
            cols[f, 0:W, :] = zero_row

    @pl.when(z + 1 < R)
    def _():
        sibling_wait(0, at1, BOT)
        for f in range(T):
            fill1(f, W + RP, W)

    @pl.when(z + 1 == R)
    def _():
        for f in range(T):
            cols[f, W + RP : EXT, :] = zero_row

    bias1 = padded(b1)
    acc = both_parts(w1)
    outs = [(v + bias1).astype(BF16).astype(F32) for v in conv_frames(*acc)]
    member_out = membership(LANES, per)
    if packed2:
        lane = lanes_of(RP)
        for f in range(T - 1):
            moved = pltpu.roll(outs[T - 1], 96 - 32 * f, 1)
            y1[t, f, W : W + RP, :] = jnp.where(lane >= 96, moved, outs[f]).astype(BF16)
    else:
        for f in range(T):
            y1[t, f, W : W + RP, :] = outs[f].astype(BF16)

    at2 = lambda src, offset, count: y1.at[src, :, pl.ds(offset, count), :]
    many2 = lambda count, offset, size: y1.at[pl.ds(0, count), :, pl.ds(offset, size), :]
    gather_start(1, at2(t, W, RP), at2(t, W, W), at2(t, RP, W), at2)
    mean, square = block_stats(outs, member_out, entries)
    held = OUT // per
    lane2 = iota2((LANES, LANES), 1)
    first = ones_where(iota2((LANES, LANES), 0) == per * lax.rem(lane2, held))
    both = group_sum(jnp.concatenate([mean, square], axis=0), first)
    chosen = iota2((2 * T, LANES), 1) // held == iota2((2 * T, LANES), 0)
    st2[me] = jnp.sum(jnp.where(chosen, both, 0.0), axis=0, keepdims=True)
    each(N - 1, lambda n: stat_copy(1, st2, n).start())

    pick = jnp.where(
        (lax.broadcasted_iota(jnp.int32, (C, LANES), 0)
         == t * OUT + lax.broadcasted_iota(jnp.int32, (C, LANES), 1))
        & (lax.broadcasted_iota(jnp.int32, (C, LANES), 1) < OUT), 1.0, 0.0).astype(BF16)
    own = jnp.dot(xin[:, W : W + RP, :].reshape(T * RP, C), pick, preferred_element_type=F32)
    pltpu.make_async_copy(aw, aw, lsem.at[11]).wait()
    mix[0] = (lax.dot_general(aw[0], aw[1], NT, preferred_element_type=F32) * C ** (-0.5)).astype(BF16)
    mix[1] = jnp.dot(aw[2], aw[3], preferred_element_type=F32).astype(BF16)

    for s in range(T):
        lane3, column = iota2((LANES, C), 0), iota2((LANES, C), 1)
        spread2[s * LANES : (s + 1) * LANES, :] = ones_where(
            (column // OUT == s) & (lax.rem(lane3, held) == lax.rem(column, OUT) // per))
    relay_rims(1, at2, (0,))
    relay(1, at2, BLK, range(1, X))
    relay_rims(1, at2, range(1, X))
    stat_all(1, st2).wait_recv()
    gain2, shift2 = flat(g2), flat(s2)
    holds = iota2((2 * T, LANES), 1) // held == iota2((2 * T, LANES), 0)
    merged = jnp.concatenate(
        [jnp.where(holds, merge_compact([st2[s * R + r] for r in range(R)], entries), 0.0) for s in range(T)], axis=1)
    wide = group_sum(merged, spread2[...])
    mean2, scale2 = wide[:T], wide[T:] * gain2

    def joined(blocks):
        return jnp.concatenate([b[:, :OUT] for b in blocks], axis=1)

    def conv_out(s, f, offset, count):
        if not packed2 or f < T - 1:
            return y1[s, f, offset : offset + count, :].astype(F32)
        lane = lanes_of(count)
        value = None
        for j in range(3):
            moved = pltpu.roll(y1[s, j, offset : offset + count, :].astype(F32), 32 + 32 * j, 1)
            value = moved if value is None else jnp.where(lane >= 32 * j, moved, value)
        return value

    def fill2(f, offset, count):
        raw = joined([conv_out(s, f, offset, count) for s in range(T)])
        value = (raw - mean2[f : f + 1]) * scale2[f : f + 1] + shift2
        put_columns(f, offset, value)

    sibling_wait(1, at2, BLK)
    for f in range(T):
        fill2(f, W, RP)
    taps_loaded(w2, 10)

    @pl.when(z > 0)
    def _():
        sibling_wait(1, at2, TOP)
        for f in range(T):
            fill2(f, 0, W)

    @pl.when(z + 1 < R)
    def _():
        sibling_wait(1, at2, BOT)
        for f in range(T):
            fill2(f, W + RP, W)

    bias2 = padded(b2)
    acc = both_parts(w2)
    for f, v in enumerate(conv_frames(*acc)):
        rounded = (v + bias2).astype(BF16).astype(F32)
        value = own[f * RP : (f + 1) * RP] + rounded
        hs[f] = (pack_rows(value) if packed3 else value).astype(BF16)

    def place(zz, tt):
        return hfull.at[zz * T + tt]

    def group(zz, count):
        return hfull.at[pl.ds(zz * T, count)]

    def hidden_start(pt, pz):
        remote(hs.at[pt], place(z, t), lsem.at[1], hid_r.at[z], pt, pz).start()

    if R == 4:
        for here, order in ((0, (2, 1)), (1, (0, 2, 3)), (2, (0, 1, 3)), (3, (0, 2))):
            @pl.when(z == here)
            def _():
                for there in order:
                    for n in range(T):
                        hidden_start(lax.rem(t + n, T), there)
        for n in range(1, T):
            hidden_start(lax.rem(t + n, T), z)
    else:
        each(N - 1, lambda n: hidden_start(*peer(n + 1)))
    hfull[z * T + t] = hs[t]

    if chained:
        by_row(row_sent, range(R))
    else:
        stat_all(0, st1).wait_send()
    gather_sent(0, at1, many1)
    stat_all(1, st2).wait_send()
    gather_sent(1, at2, many2)

    def arrived(zz, count):
        block = group(zz, count)
        remote(block, block, lsem.at[1], hid_r.at[zz], lax.rem(t + 1, T), z).wait_recv()

    def block_of(zz):
        pieces = [place(zz, s)[...].astype(F32) for s in range(T)]
        return joined([unpack_rows(p) for p in pieces] if packed3 else pieces)

    def take(zz, centre, value=None):
        value = block_of(zz) if value is None else value
        d = value - centre
        hid[pl.ds(pl.multiple_of(zz * RP, 16), RP), :] = value.astype(BF16)
        st3[...] += jnp.concatenate(
            [jnp.sum(d, axis=0, keepdims=True), jnp.sum(d * d, axis=0, keepdims=True)], axis=0)

    def forwarded(zz):
        return remote(group(zz, T), group(zz, T), lsem.at[2 + zz // 3], hid_r.at[zz], t, 3 - zz * 2 // 3)

    if R == 4:
        for here, source in ((2, 3), (2, 0)):
            @pl.when(z == here)
            def _():
                arrived(source, T)
                forwarded(source).start()

    st3[...] = jnp.zeros((2, C), F32)
    arrived(z, T - 1)
    mine_now = block_of(z)
    centre = group_sum(jnp.sum(mine_now, axis=0, keepdims=True), member) / entries
    take(z, centre, mine_now)
    if R == 4:
        for here, order in ((0, (1, 2, 3)), (1, (3, 0, 2)), (2, (0, 3, 1)), (3, (2, 1, 0))):
            @pl.when(z == here)
            def _():
                for zz in order:
                    if (here, zz) not in ((2, 0), (2, 3)):
                        arrived(zz, T)
                    take(zz, centre)
    else:
        def collect(n):
            zz = lax.rem(z + n + 1, R)
            arrived(zz, T)
            take(zz, centre)

        each(R - 1, collect)

    moments = group_sum(st3[...], member) / (entries * R)
    mean = centre + moments[0:1]
    var = moments[1:2] - moments[0:1] * moments[0:1]
    scale3 = lax.rsqrt(var + EPS) * flat(g3)
    shift3 = flat(s3)

    def normalise(r):
        part = pl.ds(pl.multiple_of(r * RP, 16), RP)
        normed[part, :] = ((hid[part, :].astype(F32) - mean) * scale3 + shift3).astype(BF16)

    each(R, normalise)
    mine = pl.ds(pl.multiple_of(z * RP, 16), RP)
    queries = jnp.dot(normed[mine, :], mix[0], preferred_element_type=F32).astype(BF16)
    scores = lax.dot_general(queries, normed[...], NT, preferred_element_type=F32)
    peak = jnp.max(scores, axis=1, keepdims=True)
    weights = jnp.exp(scores - peak)
    total = jnp.sum(weights, axis=1, keepdims=True)
    summed = jnp.dot(weights.astype(BF16), normed[...], preferred_element_type=F32)
    projected = jnp.dot(summed.astype(BF16), mix[1], preferred_element_type=F32)
    out[...] = (hid[mine, :].astype(F32) + projected / total).astype(BF16)

    def hidden_sent(count):
        most = hfull.at[pl.ds(0, count)]
        remote(most, most, lsem.at[1], hid_r.at[z], sib, z).wait_send()

    if R == 4:
        for here, source in ((2, 3), (2, 0)):
            @pl.when(z == here)
            def _():
                forwarded(source).wait_send()

        @pl.when((z == 0) | (z == 3))
        def _():
            hidden_sent(N - 1 - T)

        @pl.when((z == 1) | (z == 2))
        def _():
            hidden_sent(N - 1)
    else:
        hidden_sent(N - 1)


def solution(mesh):
    T, R = mesh.shape["tm"], mesh.shape["rows"]

    def per_device(features, g1, s1, k1, b1, g2, s2, k2, b2, g3, s3, wq, wk, wv, wo):
        _, rows, W, C = features.shape
        OUT = k1.shape[0]
        RP, EXT, N = rows * W, (rows + 2) * W, T * R
        taps = lambda k: jnp.transpose(k, (1, 2, 3, 0, 4))
        piece = 72 if OUT == 96 and RP == 96 else RP
        vmem = pl.BlockSpec(memory_space=pltpu.VMEM)
        hbm = pl.BlockSpec(memory_space=pltpu.HBM)
        dma = pltpu.SemaphoreType.DMA
        result = pl.pallas_call(
            functools.partial(kernel, T, R, W, rows, C, OUT),
            out_shape=pltpu.VMEM((RP, C), BF16),
            in_specs=[hbm] * 15,
            out_specs=vmem,
            scratch_shapes=[pltpu.VMEM((RP, C), BF16)] + [pltpu.VMEM((C,), F32)] * 6
            + [pltpu.VMEM((OUT,), F32)] * 2 + [
                pltpu.VMEM((T, EXT, C), BF16),
                pltpu.VMEM((T, 3 if T == 4 and OUT == 96 else T, EXT, LANES), BF16),
                pltpu.VMEM((T, EXT, 3 * C), BF16),
                pltpu.VMEM((3, 3, LANES, 3 * C), BF16),
                pltpu.VMEM((3, 3, LANES, 3 * C), BF16),
                pltpu.VMEM((4, C, C), BF16),
                pltpu.VMEM((N, 1, LANES), F32),
                pltpu.VMEM((N, 1, LANES), F32),
                pltpu.VMEM((2, C), F32),
                pltpu.VMEM((T, piece, LANES), BF16),
                pltpu.VMEM((N, piece, LANES), BF16),
                pltpu.VMEM((R * RP, C), BF16),
                pltpu.VMEM((R * RP, C), BF16),
                pltpu.VMEM((2, C, C), BF16),
                pltpu.VMEM((LANES, C), BF16),
                pltpu.VMEM((T * LANES, C), BF16),
                pltpu.VMEM((T, 2, C), F32),
                dma((12,)), dma((2, 3)), dma((2, 3, T)), dma((3,)), dma((R,)),
            ],
            compiler_params=pltpu.CompilerParams(
                collective_id=0, has_side_effects=True, vmem_limit_bytes=62 * 1024 * 1024),
        )(features.reshape(RP, C), g1, s1, taps(k1), b1, g2, s2,
          taps(k2), b2, g3, s3, wq, wk, wv, wo)
        return result.reshape(features.shape)

    in_specs = (
        P(("clips", "tm"), "rows", None, None), P(), P(),
        P("tm", None, None, None, None), P("tm"), P(), P(),
        P("tm", None, None, None, None), P("tm"), P(), P(), P(), P(), P(), P(),
    )
    return jax.shard_map(
        per_device, mesh=mesh, in_specs=in_specs,
        out_specs=P(("clips", "tm"), "rows", None, None), check_vma=False)
```
